32 devices in a mesh: member: 2 (over y), lon: 8 (over z, x), lat: 2 (over core).
Axes of the slice: x: 2, y: 2, z: 4, core: 2. Of those that a mesh axis runs over, the one named last changes fastest.
Arguments:
- right_side: float32 [32, 128, 256], P('member', 'lon', 'lat'), parts along dimension 0, may hold values from -5 to 5
- scale: float32 [32, 128, 256], P('member', 'lon', 'lat'), parts along dimension 0, may hold values from 0.5 to 6
- land_mask: int32 [256, 256], P(('member', 'lon'), 'lat'), parts along dimension 0, may hold values 0 or 1
- bottom: int32 [256, 256], P(('member', 'lon'), 'lat'), parts along dimension 0, may hold values from 1 to 16
Outputs:
- solution: float32 [32, 128, 256], P('member', 'lon', 'lat'), parts along dimension 0
- residual: float32 [32, 128, 256], P('member', 'lon', 'lat'), parts along dimension 0
The draws below stay inside these ranges and needn't reach their ends.
There are 2 independent parts, one for each index of `member`. The reference program is written for one: setup_inputs(seed, part) draws one part's arguments, and reference() takes and returns one part's arrays. A program takes and returns all parts, laid end to end along the dimension named above; each array names one. Nothing has to cross between parts.
All inputs are finite; a program needn't handle non-finite values. No bound on the sum of `land_mask` on one device may be relied on, other than what follows from the above.
Results may differ from the reference program's by a relative error of at most 0.0003.
Values sent between devices are 32-bit elements; how exact they have to be, the bound alone decides.
No kernel may reach another device: no remote copies, remote signals or barrier semaphores. Data moves between devices by JAX's collectives and lax.ppermute only.
A program may use at most 64 MiB of HBM per device.

```python
import math
import jax
import jax.numpy as jnp

LEV = 16
ITERS = 3
CHEB = 3
NLON = 128
NLAT = 256


def draw_right_side(key, part):
    key = jax.random.fold_in(key, 11)
    return jnp.clip(jax.random.normal(key, (LEV, NLON, NLAT), jnp.float32), -5.0, 5.0)


def draw_scale(key, part):
    key = jax.random.fold_in(key, 23)
    east_frac = jnp.arange(NLON, dtype=jnp.float32) / NLON
    ramp_factor = jnp.exp(math.log(3.0) * east_frac)[None, :, None]
    base_part = jnp.exp(jax.random.uniform(key, (LEV, NLON, NLAT), jnp.float32, math.log(0.5), math.log(2.0)))
    return base_part * ramp_factor


def with_ends(entries, rng, smallest, largest):
    place = [jax.random.randint(jax.random.fold_in(rng, axis), (), 0, length) for axis, length in enumerate(entries.shape)]
    longest = entries.shape.index(max(entries.shape))
    neighbour = place[:longest] + [(place[longest] + 1) % entries.shape[longest]] + place[longest + 1:]
    return entries.at[tuple(place)].set(smallest).at[tuple(neighbour)].set(largest)


def setup_inputs(seed: int = 0, part: int = 0) -> dict:
    splits = jax.random.split(jax.random.key(seed), 5)
    part_keys = jax.random.split(jax.random.fold_in(splits[4], part), 5)
    right_side = draw_right_side(jax.random.fold_in(jax.random.fold_in(splits[4], part), 71), part)
    scale = draw_scale(jax.random.fold_in(jax.random.fold_in(splits[4], part), 71), part)
    land_mask = with_ends((jax.random.randint(part_keys[2], (NLON, NLAT), 0, 4) < 3).astype(jnp.int32), jax.random.fold_in(part_keys[2], 1), 0, 1)
    bottom = with_ends(jax.random.randint(part_keys[3], (NLON, NLAT), 1, LEV + 1), jax.random.fold_in(part_keys[3], 1), 1, LEV).astype(jnp.int32)
    return dict(right_side=right_side, scale=scale, land_mask=land_mask, bottom=bottom)


helm_shift = 0.05
vert_ratio = 4.0
cheb_low = 4.0
cheb_high = 150.0


def cheb_factors():
    centre = 0.5 * (cheb_high + cheb_low)
    half_width = 0.5 * (cheb_high - cheb_low)
    ratio = centre / half_width
    previous = 1.0 / ratio
    factors = []
    for sweep_index in range(CHEB):
        current = 1.0 / (2.0 * ratio - previous)
        factors.append((current * previous, 2.0 * current / half_width))
        previous = current
    return centre, factors


def operator(padded_field, padded_weight):
    center = padded_field[:, 1:-1, 1:-1]
    own_weight = padded_weight[:, 1:-1, 1:-1]
    wet_cells = jnp.where(own_weight > 0.0, 1.0, 0.0).astype(own_weight.dtype)
    total = helm_shift * own_weight * center
    level_field = jnp.pad(center, ((1, 1), (0, 0), (0, 0)))
    level_weight = jnp.pad(own_weight, ((1, 1), (0, 0), (0, 0)))
    neighbours = [
        (padded_field[:, 2:, 1:-1], padded_weight[:, 2:, 1:-1], 0.5),
        (padded_field[:, :-2, 1:-1], padded_weight[:, :-2, 1:-1], 0.5),
        (padded_field[:, 1:-1, 2:], padded_weight[:, 1:-1, 2:], 0.5),
        (padded_field[:, 1:-1, :-2], padded_weight[:, 1:-1, :-2], 0.5),
        (level_field[2:], level_weight[2:], 0.5 * vert_ratio),
        (level_field[:-2], level_weight[:-2], 0.5 * vert_ratio),
    ]
    for other_field, other_weight, factor in neighbours:
        conduct = jnp.where(other_weight > 0.0, factor * (own_weight + other_weight), 0.0)
        total = total + conduct * (center - other_field)
    return wet_cells * total + (1.0 - wet_cells) * center


def pad_both(values):
    wrapped = jnp.pad(values, ((0, 0), (1, 1), (0, 0)), mode="wrap")
    return jnp.pad(wrapped, ((0, 0), (0, 0), (1, 1)))


def reference(right_side, scale, land_mask, bottom):
    levels = jnp.arange(LEV, dtype=jnp.int32)[:, None, None]
    wet = jnp.where((land_mask[None] == 1) & (levels < bottom[None]), 1.0, 0.0).astype(jnp.float32)
    cell_weight = wet * scale
    source = wet * right_side
    weight_pad = pad_both(cell_weight)
    centre, factors = cheb_factors()

    def apply_op(values):
        return operator(pad_both(values), weight_pad)

    def smooth(values):
        update = values / centre
        iterate = update
        for first, second in factors:
            defect = values - apply_op(iterate)
            update = first * update + second * defect
            iterate = iterate + update
        return iterate

    residual = source
    smoothed = smooth(residual)
    applied = apply_op(smoothed)
    solution = jnp.zeros_like(source)
    dir_applied = jnp.zeros_like(source)
    dir_smoothed = jnp.zeros_like(source)
    dir_image = jnp.zeros_like(source)
    direction = jnp.zeros_like(source)
    gamma_prev = None
    alpha_prev = None
    for turn_index in range(ITERS):
        gamma_now = jnp.sum(residual * smoothed)
        delta_now = jnp.sum(applied * smoothed)
        smoothed_new = smooth(applied)
        applied_new = apply_op(smoothed_new)
        if turn_index == 0:
            beta_now = jnp.float32(0.0)
            alpha_now = gamma_now / delta_now
        else:
            beta_now = gamma_now / gamma_prev
            alpha_now = gamma_now / (delta_now - beta_now * gamma_now / alpha_prev)
        dir_applied = applied_new + beta_now * dir_applied
        dir_smoothed = smoothed_new + beta_now * dir_smoothed
        dir_image = applied + beta_now * dir_image
        direction = smoothed + beta_now * direction
        solution = solution + alpha_now * direction
        residual = residual - alpha_now * dir_image
        smoothed = smoothed - alpha_now * dir_smoothed
        applied = applied - alpha_now * dir_applied
        gamma_prev = gamma_now
        alpha_prev = alpha_now
    return solution, residual
```

```python
import functools

import jax
import jax.numpy as jnp
from jax import lax
from jax.experimental import pallas as pl
from jax.experimental.pallas import tpu as pltpu
from jax.sharding import PartitionSpec as P

ITERS = 3
CHEB = 3
DEPTH = ITERS * (CHEB + 1)
STRIP = 16
SEGS = 8
SUB = 8
LANES = 128

helm_shift = 0.05
vert_ratio = 4.0
cheb_low = 4.0
cheb_high = 150.0

CENTRE = 0.5 * (cheb_high + cheb_low)
HALF = 0.5 * (cheb_high - cheb_low)
MU = CENTRE / HALF
NU = MU * MU - 1.0
STEP = 5.0
VMEM_BYTES = 48 * 1024 * 1024


def prep_kernel(core_ref, right_ref, scale_ref, land_ref, bottom_ref, own_ref, fwd_ref, bwd_ref, strip_ref):
    rows = land_ref.shape[0]
    core = core_ref[0]
    sub = lax.broadcasted_iota(jnp.int32, (SUB, LANES), 0)
    lane = lax.broadcasted_iota(jnp.int32, (SUB, LANES), 1)
    for group in range(rows // SEGS):
        packed = {}
        for seg in range(SEGS):
            i = group * SEGS + seg
            sea = land_ref[i : i + 1, :] == 1
            deep = jnp.where(sea, bottom_ref[i : i + 1, :], 0)
            deep = jnp.broadcast_to(deep, (SUB, LANES))
            shift = lax.rem(STRIP * seg + STRIP * (1 - core), LANES)
            for par in range(2):
                wet = 2 * sub + par < deep
                at = pl.ds(par * rows + i, SUB, stride=2 * rows)
                for f, ref in enumerate((scale_ref, right_ref)):
                    x = jnp.where(wet, ref[at, :], 0.0)
                    own_ref[i, f, par] = x
                    if i >= rows - DEPTH:
                        fwd_ref[i - (rows - DEPTH), f, par] = x
                    if i < DEPTH:
                        bwd_ref[i, f, par] = x
                    y = pltpu.roll(x, shift, 1)
                    if seg == 0:
                        packed[f, par] = y
                    else:
                        packed[f, par] = jnp.where(lane >= STRIP * seg, y, packed[f, par])
        for (f, par), y in packed.items():
            strip_ref[group, f, par] = y


def prep(core, right, scale, land, bottom):
    rows = land.shape[0]
    out = lambda n: jax.ShapeDtypeStruct((n, 2, 2, SUB, LANES), jnp.float32)
    vmem = pl.BlockSpec(memory_space=pltpu.VMEM)
    return pl.pallas_call(
        prep_kernel,
        out_shape=(out(rows), out(DEPTH), out(DEPTH), out(rows // SEGS)),
        in_specs=[pl.BlockSpec(memory_space=pltpu.SMEM)] + [vmem] * 4,
        out_specs=(vmem,) * 4,
        compiler_params=pltpu.CompilerParams(vmem_limit_bytes=VMEM_BYTES),
        name="prep",
    )(core, right, scale, land, bottom)


def main_kernel(
    core_ref, own_ref, west_ref, east_ref, strip_ref, strip_w_ref, strip_e_ref,
    u_ref, r_ref, part_ref,
    w_ref, v_ref, p_ref, q_ref, ce_ref, cn_ref, ca_ref, cb_ref, d1_ref, d0_ref, hw_ref,
):
    rows = own_ref.shape[0]
    total = rows + 2 * DEPTH
    core = core_ref[0]
    sub = lax.broadcasted_iota(jnp.int32, (SUB, LANES), 0)
    lane = lax.broadcasted_iota(jnp.int32, (SUB, LANES), 1)
    base = core * (LANES - STRIP)
    in_strip = (lane >= base) & (lane < base + STRIP)
    first_lane = lane == 0
    last_lane = lane == LANES - 1

    def unpack(r, f, par):
        row = r - DEPTH
        if row < 0:
            ref, k, row = west_ref, r, row + rows
            strips = strip_w_ref
        elif row < rows:
            ref, k = own_ref, row
            strips = strip_ref
        else:
            ref, k, row = east_ref, row - rows, row - rows
            strips = strip_e_ref
        shift = lax.rem(base + (LANES - STRIP * (row % SEGS)), LANES)
        far = pltpu.roll(strips[row // SEGS, f, par], shift, 1)
        return ref[k, f, par], jnp.where(in_strip, far, 0.0)

    for r in range(total):
        for par in range(2):
            for f, ref in enumerate((w_ref, v_ref)):
                near, far = unpack(r, f, par)
                ref[r, par] = near
                ref[r, 2 + par] = far

    def north(x):
        a, b = (pltpu.roll(t, LANES - 1, 1) for t in x)
        return jnp.where(last_lane, b, a), jnp.where(last_lane, a, b)

    def south(x):
        a, b = (pltpu.roll(t, 1, 1) for t in x)
        return jnp.where(first_lane, b, a), jnp.where(first_lane, a, b)

    def up(x):
        return pltpu.roll(x, SUB - 1, 0)

    def down(x):
        return pltpu.roll(x, 1, 0)

    def conduct(x, y, factor):
        return jnp.where(jnp.minimum(x, y) > 0.0, (x + y) * (factor / HALF), 0.0)

    def coefs(r, _):
        w = [w_ref[r, t] for t in range(4)]
        ahead = jnp.minimum(r + 1, total - 1)
        for t in range(4):
            ce_ref[r, t] = conduct(w[t], w_ref[ahead, t], 0.5)
            hw = w[t] * (helm_shift / HALF)
            hw_ref[r, t] = hw
            d0_ref[r, t] = MU - hw
            d1_ref[r, t] = 2.0 * MU - hw
        for par in range(2):
            x = (w[par], w[2 + par])
            for side, y in enumerate(north(x)):
                cn_ref[r, 2 * side + par] = conduct(x[side], y, 0.5)
        for side in range(2):
            even, odd = w[2 * side], w[2 * side + 1]
            ca_ref[r, side] = conduct(even, odd, 0.5 * vert_ratio)
            above = jnp.where(sub == SUB - 1, 0.0, up(even))
            cb_ref[r, side] = conduct(odd, above, 0.5 * vert_ratio)
        return 0

    lax.fori_loop(0, total, coefs, 0)

    def apply(src, dst, level, finish):
        def row_step(r, now, flux_w):
            ahead = [src[r + 1, t] for t in range(4)]
            flux_e = [ce_ref[r, t] * (ahead[t] - now[t]) for t in range(4)]
            acc = [flux_e[t] - flux_w[t] for t in range(4)]
            for par in range(2):
                x = (now[par], now[2 + par])
                n = north(x)
                flux = [cn_ref[r, 2 * s + par] * (n[s] - x[s]) for s in range(2)]
                back = south(flux)
                for s in range(2):
                    acc[2 * s + par] = acc[2 * s + par] + (flux[s] - back[s])
            for s in range(2):
                even, odd = now[2 * s], now[2 * s + 1]
                fa = ca_ref[r, s] * (odd - even)
                fb = cb_ref[r, s] * (up(even) - odd)
                acc[2 * s] = acc[2 * s] + (fa - down(fb))
                acc[2 * s + 1] = acc[2 * s + 1] + (fb - fa)
            for t in range(4):
                dst[r, t] = finish(r, t, acc[t], now[t])
            return ahead, flux_e

        now = [src[level, t] for t in range(4)]
        flux_w = [ce_ref[level - 1, t] * (now[t] - src[level - 1, t]) for t in range(4)]

        def body(k, carry):
            now, flux_w = carry[:4], carry[4:]
            r = level + 2 * k
            now, flux_w = row_step(r, now, flux_w)
            now, flux_w = row_step(r + 1, now, flux_w)
            return tuple(now) + tuple(flux_w)

        lax.fori_loop(0, (total - 2 * level) // 2, body, tuple(now) + tuple(flux_w))

    def dots(k, left):
        acc = jnp.zeros((SUB, LANES), jnp.float32)
        for i in range(rows):
            for par in range(2):
                acc = acc + left(i, par) * u_ref[k, i, par]
        return jnp.sum(acc, axis=0, keepdims=True)

    parts = []
    for k in range(ITERS):
        level = k * (CHEB + 1)
        apply(v_ref, p_ref, level + 1, lambda r, t, g, x: g + d1_ref[r, t] * x)
        apply(p_ref, q_ref, level + 2, lambda r, t, g, x: g + d0_ref[r, t] * x + NU * v_ref[r, t])
        apply(q_ref, p_ref, level + 3, lambda r, t, g, x: g + d0_ref[r, t] * x + MU * NU * v_ref[r, t])
        for i in range(rows):
            for par in range(2):
                u_ref[k, i, par] = p_ref[i + DEPTH, par]
        parts.append(dots(k, lambda i, par: v_ref[i + DEPTH, par]))
        apply(p_ref, v_ref, level + 4, lambda r, t, g, x: v_ref[r, t] - STEP * (hw_ref[r, t] * x - g))
        for i in range(rows):
            for par in range(2):
                r_ref[k, i, par] = v_ref[i + DEPTH, par]
        parts.append(dots(k, lambda i, par: v_ref[i + DEPTH, par]))
    block = jnp.zeros((SUB, LANES), jnp.float32)
    for j, part in enumerate(parts):
        block = jnp.where(sub == j, part, block)
    for n in range(part_ref.shape[0]):
        part_ref[n] = block


def main(core, own, west, east, strip, strip_w, strip_e, peers):
    rows = own.shape[0]
    total = rows + 2 * DEPTH
    vmem = pl.BlockSpec(memory_space=pltpu.VMEM)
    field = jax.ShapeDtypeStruct((ITERS, rows, 2, SUB, LANES), jnp.float32)
    full = pltpu.VMEM((total, 4, SUB, LANES), jnp.float32)
    half = pltpu.VMEM((total, 2, SUB, LANES), jnp.float32)
    return pl.pallas_call(
        main_kernel,
        out_shape=(field, field, jax.ShapeDtypeStruct((peers, SUB, LANES), jnp.float32)),
        in_specs=[pl.BlockSpec(memory_space=pltpu.SMEM)] + [vmem] * 6,
        out_specs=(vmem,) * 3,
        scratch_shapes=[full] * 6 + [half] * 2 + [full] * 3,
        compiler_params=pltpu.CompilerParams(vmem_limit_bytes=VMEM_BYTES),
        name="krylov",
    )(core, own, west, east, strip, strip_w, strip_e)


def times_t(poly):
    out = [poly[0]]
    for i in range(1, len(poly)):
        out.append(poly[i] - poly[i - 1])
    out.append(-poly[-1])
    return out


def add_scaled(left, factor, right):
    out = []
    for i in range(max(len(left), len(right))):
        if i >= len(right):
            out.append(left[i])
        elif i >= len(left):
            out.append(factor * right[i])
        else:
            out.append(left[i] + factor * right[i])
    return out


def inner(left, right, moments):
    total = None
    for i, x in enumerate(left):
        for j, y in enumerate(right):
            term = x * y * moments[i + j]
            total = term if total is None else total + term
    return total


def last_kernel(sums_ref, own_ref, u_ref, r_ref, sol_ref, res_ref):
    rows = own_ref.shape[0]
    peers = sums_ref.shape[0]
    acc = sums_ref[0]
    for n in range(1, peers):
        acc = acc + sums_ref[n]
    sums = jnp.broadcast_to(jnp.sum(acc, axis=1, keepdims=True), (SUB, LANES))
    moments = [jnp.broadcast_to(sums[j : j + 1, :], (SUB, LANES)) for j in range(2 * ITERS)]
    res = [jnp.ones((SUB, LANES), jnp.float32)]
    direction = res
    sol = None
    gamma = alpha = None
    for turn in range(ITERS):
        gamma_now = inner(res, res, moments)
        delta = inner(times_t(res), res, moments)
        if turn == 0:
            alpha = gamma_now / delta
            sol = [alpha]
        else:
            beta = gamma_now / gamma
            alpha = gamma_now / (delta - beta * gamma_now / alpha)
            direction = add_scaled(res, beta, direction)
            sol = add_scaled(sol, alpha, direction)
        res = add_scaled(res, -alpha, times_t(direction))
        gamma = gamma_now
    sol = [x * (STEP / HALF) for x in sol]
    for i in range(rows):
        for par in range(2):
            at = pl.ds(par * rows + i, SUB, stride=2 * rows)
            x = sol[0] * u_ref[0, i, par]
            y = res[0] * own_ref[i, 1, par]
            for k in range(ITERS):
                if k:
                    x = x + sol[k] * u_ref[k, i, par]
                y = y + res[k + 1] * r_ref[k, i, par]
            sol_ref[at, :] = x
            res_ref[at, :] = y


def last(sums, own, u, r):
    rows = own.shape[0]
    vmem = pl.BlockSpec(memory_space=pltpu.VMEM)
    out = jax.ShapeDtypeStruct((2 * SUB * rows, LANES), jnp.float32)
    return pl.pallas_call(
        last_kernel,
        out_shape=(out, out),
        in_specs=[vmem] * 4,
        out_specs=(vmem,) * 2,
        compiler_params=pltpu.CompilerParams(vmem_limit_bytes=VMEM_BYTES),
        name="combine",
    )(sums, own, u, r)


def local(right_side, scale, land_mask, bottom):
    levels, rows, lats = right_side.shape
    lon = lax.axis_size("lon")
    lat = lax.axis_size("lat")
    assert levels == 2 * SUB and lats == LANES and lat == 2
    assert rows % SEGS == 0 and rows >= DEPTH and STRIP >= DEPTH
    both = ("lon", "lat")
    place = lambda i, j: (i % lon) * lat + j
    east = [(place(i, j), place(i + 1, j)) for i in range(lon) for j in range(lat)]
    west = [(place(i, j), place(i - 1, j)) for i in range(lon) for j in range(lat)]
    east_x = [(place(i, j), place(i + 1, 1 - j)) for i in range(lon) for j in range(lat)]
    west_x = [(place(i, j), place(i - 1, 1 - j)) for i in range(lon) for j in range(lat)]
    beside = [(place(i, j), place(i, 1 - j)) for i in range(lon) for j in range(lat)]

    core = lax.axis_index("lat").astype(jnp.int32).reshape(1)
    own, fwd, bwd, strip = prep(
        core,
        right_side.reshape(levels * rows, lats),
        scale.reshape(levels * rows, lats),
        land_mask,
        bottom,
    )
    from_west = lax.ppermute(fwd, both, east)
    from_east = lax.ppermute(bwd, both, west)
    strip_w = lax.ppermute(strip, both, east_x)
    strip_e = lax.ppermute(strip, both, west_x)
    strip_o = lax.ppermute(strip, both, beside)
    u, r, parts = main(core, own, from_west, from_east, strip_o, strip_w, strip_e, lon * lat)
    sums = lax.all_to_all(parts, both, 0, 0)
    sol, res = last(sums, own, u, r)
    return sol.reshape(right_side.shape), res.reshape(right_side.shape)


def solution(mesh):
    field = P("member", "lon", "lat")
    mask = P(("member", "lon"), "lat")
    return jax.shard_map(
        local,
        mesh=mesh,
        in_specs=(field, field, mask, mask),
        out_specs=(field, field),
        check_vma=False,
    )
```

```python
import functools

import jax
import jax.numpy as jnp
from jax import lax
from jax.experimental import pallas as pl
from jax.experimental.pallas import tpu as pltpu
from jax.sharding import PartitionSpec as P

ITERS = 3
CHEB = 3
DEPTH = ITERS * (CHEB + 1)
SUB = 8
LANES = 128
WIDE = LANES // 2
SEGS = 8
EDGE = WIDE // SEGS

helm_shift = 0.05
vert_ratio = 4.0
cheb_low = 4.0
cheb_high = 150.0

CENTRE = 0.5 * (cheb_high + cheb_low)
HALF = 0.5 * (cheb_high - cheb_low)
MU = CENTRE / HALF
NU = MU * MU - 1.0
STEP = 5.0
VMEM_BYTES = 48 * 1024 * 1024


def take_lanes(x, index):
    return jnp.take_along_axis(x, index, axis=1, mode="promise_in_bounds")


def prep_kernel(core_ref, *refs):
    sources, (own_ref, fwd_ref, bwd_ref, strip_ref), held, sems = refs[:4], refs[4:8], refs[8:12], refs[12]
    copies = [pltpu.make_async_copy(a, b, sems.at[k]) for k, (a, b) in enumerate(zip(sources, held))]
    for copy in copies:
        copy.start()
    for copy in copies:
        copy.wait()
    right_ref, scale_ref, land_ref, bottom_ref = held
    rows = land_ref.shape[0]
    core = core_ref[0]
    sub = lax.broadcasted_iota(jnp.int32, (SUB, LANES), 0)
    lane = lax.broadcasted_iota(jnp.int32, (SUB, LANES), 1)
    half_lane = lane % WIDE
    apart = 2 * half_lane + lane // WIDE
    for group in range(rows // SEGS):
        packed = {}
        for seg in range(SEGS):
            i = group * SEGS + seg
            sea = land_ref[i : i + 1, :] == 1
            deep = jnp.where(sea, bottom_ref[i : i + 1, :], 0)
            deep = jnp.broadcast_to(deep, (SUB, LANES))
            shift = lax.rem(EDGE * seg + (1 - core) * (WIDE + EDGE), LANES)
            for par in range(2):
                wet = 2 * sub + par < deep
                at = pl.ds(par * rows + i, SUB, stride=2 * rows)
                for f, ref in enumerate((scale_ref, right_ref)):
                    x = take_lanes(jnp.where(wet, ref[at, :], 0.0), apart)
                    own_ref[i, f, par] = x
                    if i >= rows - DEPTH:
                        fwd_ref[i - (rows - DEPTH), f, par] = x
                    if i < DEPTH:
                        bwd_ref[i, f, par] = x
                    y = pltpu.roll(x, shift, 1)
                    if seg == 0:
                        packed[f, par] = y
                    else:
                        packed[f, par] = jnp.where(half_lane >= EDGE * seg, y, packed[f, par])
        for (f, par), y in packed.items():
            strip_ref[group, f, par] = y


def prep(core, right, scale, land, bottom):
    rows = land.shape[0]
    out = lambda n: jax.ShapeDtypeStruct((n, 2, 2, SUB, LANES), jnp.float32)
    vmem = pl.BlockSpec(memory_space=pltpu.VMEM)
    return pl.pallas_call(
        prep_kernel,
        out_shape=(out(rows), out(DEPTH), out(DEPTH), out(rows // SEGS)),
        in_specs=[pl.BlockSpec(memory_space=pltpu.SMEM)] + [pl.BlockSpec(memory_space=pltpu.HBM)] * 4,
        out_specs=(vmem,) * 4,
        scratch_shapes=[pltpu.VMEM(x.shape, x.dtype) for x in (right, scale, land, bottom)]
        + [pltpu.SemaphoreType.DMA((4,))],
        compiler_params=pltpu.CompilerParams(vmem_limit_bytes=63 * 1024 * 1024),
        name="prep",
    )(core, right, scale, land, bottom)


def main_kernel(
    core_ref, own_ref, west_ref, east_ref, strip_ref, strip_w_ref, strip_e_ref,
    u_ref, r_ref, part_ref,
    w_ref, v_ref, p_ref, q_ref, ce_ref, cn_ref, cl_ref, ca_ref, cb_ref, d1_ref, d0_ref, hw_ref,
):
    rows = own_ref.shape[0]
    total = rows + 2 * DEPTH
    core = core_ref[0]
    sub = lax.broadcasted_iota(jnp.int32, (SUB, LANES), 0)
    lane = lax.broadcasted_iota(jnp.int32, (SUB, LANES), 1)
    base = WIDE + core * (WIDE - EDGE)
    left = lane < WIDE
    in_even = (lane >= base) & (lane < base + EDGE)
    in_odd = (lane >= base - WIDE) & (lane < base - WIDE + EDGE)

    def unpack(r, f, par):
        row = r - DEPTH
        if row < 0:
            ref, k, row = west_ref, r, row + rows
            strips = strip_w_ref
        elif row < rows:
            ref, k = own_ref, row
            strips = strip_ref
        else:
            ref, k, row = east_ref, row - rows, row - rows
            strips = strip_e_ref
        shift = lax.rem(base + (LANES - EDGE * (row % SEGS)), LANES)
        far = pltpu.roll(strips[row // SEGS, f, par], shift, 1)
        near = ref[k, f, par]
        even = jnp.where(left, near, jnp.where(in_even, far, 0.0))
        odd = jnp.where(left, jnp.where(in_odd, far, 0.0), near)
        return even, pltpu.roll(odd, WIDE, 1)

    for r in range(total):
        for par in range(2):
            for f, ref in enumerate((w_ref, v_ref)):
                even, odd = unpack(r, f, par)
                ref[r, par] = even
                ref[r, 2 + par] = odd

    def north(x):
        return pltpu.roll(x, LANES - 1, 1)

    def south(x):
        return pltpu.roll(x, 1, 1)

    def up(x):
        return pltpu.roll(x, SUB - 1, 0)

    def down(x):
        return pltpu.roll(x, 1, 0)

    def conduct(x, y, factor):
        return jnp.where(jnp.minimum(x, y) > 0.0, (x + y) * (factor / HALF), 0.0)

    def coefs(r):
        w = [w_ref[r, t] for t in range(4)]
        ahead = min(r + 1, total - 1)
        lat = [None] * 4
        for par in range(2):
            even, odd = w[par], w[2 + par]
            cl_ref[r, par] = conduct(even, odd, 0.5)
            lat[2 + par] = conduct(odd, north(even), 0.5)
            lat[par] = south(lat[2 + par])
            cn_ref[r, par] = lat[par]
            cn_ref[r, 2 + par] = lat[2 + par]
        for side in range(2):
            even, odd = w[2 * side], w[2 * side + 1]
            ca_ref[r, side] = conduct(even, odd, 0.5 * vert_ratio)
            above = jnp.where(sub == SUB - 1, 0.0, up(even))
            cb = conduct(odd, above, 0.5 * vert_ratio)
            cb_ref[r, 2 * side] = down(cb)
            cb_ref[r, 2 * side + 1] = cb
            lat[2 * side] = lat[2 * side] + down(cb)
            lat[2 * side + 1] = lat[2 * side + 1] + cb
        for t in range(4):
            ce_ref[r, t] = conduct(w[t], w_ref[ahead, t], 0.5)
            hw = w[t] * (helm_shift / HALF) + lat[t]
            hw_ref[r, t] = hw
            d0_ref[r, t] = MU - hw
            d1_ref[r, t] = 2.0 * MU - hw

    for r in range(total):
        coefs(r)

    def apply(src, dst, level, finish):
        last_flux = [ce_ref[level - 1, t] * (src[level, t] - src[level - 1, t]) for t in range(4)]
        now = [src[level, t] for t in range(4)]
        for r in range(level, total - level):
            ahead = [src[r + 1, t] for t in range(4)]
            flux = [ce_ref[r, t] * (ahead[t] - now[t]) for t in range(4)]
            acc = [flux[t] - last_flux[t] for t in range(4)]
            for par in range(2):
                even, odd = now[par], now[2 + par]
                fl = cl_ref[r, par] * (odd - even)
                acc[par] = acc[par] + (cn_ref[r, par] * south(odd) + fl)
                acc[2 + par] = acc[2 + par] + (cn_ref[r, 2 + par] * north(even) - fl)
            for s in range(2):
                even, odd = now[2 * s], now[2 * s + 1]
                fa = ca_ref[r, s] * (odd - even)
                acc[2 * s] = acc[2 * s] + (cb_ref[r, 2 * s] * down(odd) + fa)
                acc[2 * s + 1] = acc[2 * s + 1] + (cb_ref[r, 2 * s + 1] * up(even) - fa)
            for t in range(4):
                dst[r, t] = finish(r, t, acc[t], now[t])
            now, last_flux = ahead, flux

    def dots(k, other):
        acc = jnp.zeros((SUB, LANES), jnp.float32)
        for i in range(rows):
            for t in range(4):
                acc = acc + other(i, t) * u_ref[k, i, t]
        return jnp.sum(jnp.where(left, acc, 0.0), axis=0, keepdims=True)

    parts = []
    for k in range(ITERS):
        level = k * (CHEB + 1)
        apply(v_ref, p_ref, level + 1, lambda r, t, g, x: g + d1_ref[r, t] * x)
        apply(p_ref, q_ref, level + 2, lambda r, t, g, x: g + d0_ref[r, t] * x + NU * v_ref[r, t])
        apply(q_ref, p_ref, level + 3, lambda r, t, g, x: g + d0_ref[r, t] * x + MU * NU * v_ref[r, t])
        for i in range(rows):
            for t in range(4):
                u_ref[k, i, t] = p_ref[i + DEPTH, t]
        parts.append(dots(k, lambda i, t: v_ref[i + DEPTH, t]))
        apply(p_ref, v_ref, level + 4, lambda r, t, g, x: v_ref[r, t] - STEP * (hw_ref[r, t] * x - g))
        for i in range(rows):
            for t in range(4):
                r_ref[k, i, t] = v_ref[i + DEPTH, t]
        parts.append(dots(k, lambda i, t: v_ref[i + DEPTH, t]))
    block = jnp.zeros((SUB, LANES), jnp.float32)
    for j, part in enumerate(parts):
        block = jnp.where(sub == j, part, block)
    for n in range(part_ref.shape[0]):
        part_ref[n] = block


def main(core, own, west, east, strip, strip_w, strip_e, peers):
    rows = own.shape[0]
    total = rows + 2 * DEPTH
    vmem = pl.BlockSpec(memory_space=pltpu.VMEM)
    field = jax.ShapeDtypeStruct((ITERS, rows, 4, SUB, LANES), jnp.float32)
    full = pltpu.VMEM((total, 4, SUB, LANES), jnp.float32)
    half = pltpu.VMEM((total, 2, SUB, LANES), jnp.float32)
    return pl.pallas_call(
        main_kernel,
        out_shape=(field, field, jax.ShapeDtypeStruct((peers, SUB, LANES), jnp.float32)),
        in_specs=[pl.BlockSpec(memory_space=pltpu.SMEM)] + [vmem] * 6,
        out_specs=(vmem,) * 3,
        scratch_shapes=[full] * 6 + [half] * 2 + [full] * 4,
        compiler_params=pltpu.CompilerParams(vmem_limit_bytes=VMEM_BYTES),
        name="krylov",
    )(core, own, west, east, strip, strip_w, strip_e)


def times_t(poly):
    out = [poly[0]]
    for i in range(1, len(poly)):
        out.append(poly[i] - poly[i - 1])
    out.append(-poly[-1])
    return out


def add_scaled(left, factor, right):
    out = []
    for i in range(max(len(left), len(right))):
        if i >= len(right):
            out.append(left[i])
        elif i >= len(left):
            out.append(factor * right[i])
        else:
            out.append(left[i] + factor * right[i])
    return out


def inner(left, right, moments):
    total = None
    for i, x in enumerate(left):
        for j, y in enumerate(right):
            term = x * y * moments[i + j]
            total = term if total is None else total + term
    return total


def last_kernel(sums_ref, own_ref, u_ref, r_ref, sol_ref, res_ref):
    rows = own_ref.shape[0]
    peers = sums_ref.shape[0]
    acc = sums_ref[0]
    for n in range(1, peers):
        acc = acc + sums_ref[n]
    sums = jnp.broadcast_to(jnp.sum(acc, axis=1, keepdims=True), (SUB, LANES))
    moments = [jnp.broadcast_to(sums[j : j + 1, :], (SUB, LANES)) for j in range(2 * ITERS)]
    res = [jnp.ones((SUB, LANES), jnp.float32)]
    direction = res
    sol = None
    gamma = alpha = None
    for turn in range(ITERS):
        gamma_now = inner(res, res, moments)
        delta = inner(times_t(res), res, moments)
        if turn == 0:
            alpha = gamma_now / delta
            sol = [alpha]
        else:
            beta = gamma_now / gamma
            alpha = gamma_now / (delta - beta * gamma_now / alpha)
            direction = add_scaled(res, beta, direction)
            sol = add_scaled(sol, alpha, direction)
        res = add_scaled(res, -alpha, times_t(direction))
        gamma = gamma_now
    sol = [x * (STEP / HALF) for x in sol]
    lane = lax.broadcasted_iota(jnp.int32, (SUB, LANES), 1)
    left = lane < WIDE
    mixed = WIDE * (lane % 2) + lane // 2
    for i in range(rows):
        for par in range(2):
            at = pl.ds(par * rows + i, SUB, stride=2 * rows)
            pair = []
            for t in (par, 2 + par):
                x = sol[0] * u_ref[0, i, t]
                y = res[1] * r_ref[0, i, t]
                for k in range(1, ITERS):
                    x = x + sol[k] * u_ref[k, i, t]
                    y = y + res[k + 1] * r_ref[k, i, t]
                pair.append((x, y))
            x, y = (jnp.where(left, even, pltpu.roll(odd, WIDE, 1)) for even, odd in zip(*pair))
            x = take_lanes(x, mixed)
            y = take_lanes(y + res[0] * own_ref[i, 1, par], mixed)
            sol_ref[at, :] = x
            res_ref[at, :] = y


def last(sums, own, u, r):
    rows = own.shape[0]
    vmem = pl.BlockSpec(memory_space=pltpu.VMEM)
    out = jax.ShapeDtypeStruct((2 * SUB * rows, LANES), jnp.float32)
    return pl.pallas_call(
        last_kernel,
        out_shape=(out, out),
        in_specs=[vmem] * 4,
        out_specs=(vmem,) * 2,
        compiler_params=pltpu.CompilerParams(vmem_limit_bytes=VMEM_BYTES),
        name="combine",
    )(sums, own, u, r)


def local(right_side, scale, land_mask, bottom):
    levels, rows, lats = right_side.shape
    lon = lax.axis_size("lon")
    lat = lax.axis_size("lat")
    assert levels == 2 * SUB and lats == LANES and lat == 2
    assert rows % SEGS == 0 and rows >= DEPTH and 2 * EDGE >= DEPTH
    both = ("lon", "lat")
    place = lambda i, j: (i % lon) * lat + j
    east = [(place(i, j), place(i + 1, j)) for i in range(lon) for j in range(lat)]
    west = [(place(i, j), place(i - 1, j)) for i in range(lon) for j in range(lat)]
    east_x = [(place(i, j), place(i + 1, 1 - j)) for i in range(lon) for j in range(lat)]
    west_x = [(place(i, j), place(i - 1, 1 - j)) for i in range(lon) for j in range(lat)]
    beside = [(place(i, j), place(i, 1 - j)) for i in range(lon) for j in range(lat)]

    core = lax.axis_index("lat").astype(jnp.int32).reshape(1)
    own, fwd, bwd, strip = prep(
        core,
        right_side.reshape(levels * rows, lats),
        scale.reshape(levels * rows, lats),
        land_mask,
        bottom,
    )
    from_west = lax.ppermute(fwd, both, east)
    from_east = lax.ppermute(bwd, both, west)
    strip_w = lax.ppermute(strip, both, east_x)
    strip_e = lax.ppermute(strip, both, west_x)
    strip_o = lax.ppermute(strip, both, beside)
    u, r, parts = main(core, own, from_west, from_east, strip_o, strip_w, strip_e, lon * lat)
    sums = lax.all_to_all(parts, both, 0, 0)
    sol, res = last(sums, own, u, r)
    return sol.reshape(right_side.shape), res.reshape(right_side.shape)


def solution(mesh):
    field = P("member", "lon", "lat")
    mask = P(("member", "lon"), "lat")
    return jax.shard_map(
        local,
        mesh=mesh,
        in_specs=(field, field, mask, mask),
        out_specs=(field, field),
        check_vma=False,
    )
```

```python
import functools

import jax
import jax.numpy as jnp
from jax import lax
from jax.experimental import pallas as pl
from jax.experimental.pallas import tpu as pltpu
from jax.sharding import PartitionSpec as P

ITERS = 3
CHEB = 3
DEPTH = ITERS * (CHEB + 1)
SUB = 8
LANES = 128
WIDE = LANES // 2
SEGS = 8
EDGE = WIDE // SEGS

helm_shift = 0.05
vert_ratio = 4.0
cheb_low = 4.0
cheb_high = 150.0

CENTRE = 0.5 * (cheb_high + cheb_low)
HALF = 0.5 * (cheb_high - cheb_low)
MU = CENTRE / HALF
NU = MU * MU - 1.0
STEP = 5.0
NAMES = ("ce", "cn", "cl", "ca", "cb", "d1", "d0", "hw")
TILES = dict(ce=4, cn=4, cl=2, ca=2, cb=4, d1=4, d0=4, hw=4)
EVERY = CHEB + 1
SPARE = 2
MIB = 1024 * 1024


def take_lanes(x, index):
    return jnp.take_along_axis(x, index, axis=1, mode="promise_in_bounds")


def spread(ref, index, tiles):
    for t, tile in enumerate(tiles):
        ref[index + (t,)] = tile


def iotas():
    sub = lax.broadcasted_iota(jnp.int32, (SUB, LANES), 0)
    lane = lax.broadcasted_iota(jnp.int32, (SUB, LANES), 1)
    return sub, lane


def column(rows, r, flip):
    return r + flip * (rows - 1 - 2 * r)


def spare_lanes(core):
    _, lane = iotas()
    back = lax.rem(EDGE - SPARE + core * (LANES - 2 * (EDGE - SPARE)), LANES)
    start = (1 - core) * (EDGE - SPARE)
    in_slot = lane % EDGE
    return (in_slot >= start) & (in_slot < start + SPARE), back


def prep_kernel(place_ref, right_ref, scale_ref, own_ref, strip_ref, near_ref, corner_ref):
    rows = own_ref.shape[0]
    core, flip = place_ref[0] % 2, place_ref[0] // 2
    _, lane = iotas()
    half_lane = lane % WIDE
    apart = 2 * half_lane + lane // WIDE
    packed = {}
    for r in range(rows):
        group, seg = divmod(r, SEGS)
        shift = lax.rem(EDGE * seg + (1 - core) * (WIDE + EDGE), LANES)
        for par in range(2):
            at = pl.ds(par * rows + column(rows, r, flip), SUB, stride=2 * rows)
            for f, ref in enumerate((scale_ref, right_ref)):
                x = take_lanes(ref[at, :], apart)
                own_ref[r, f, par] = x
                if r < DEPTH:
                    near_ref[r, f, par] = x
                y = pltpu.roll(x, shift, 1)
                if seg:
                    y = jnp.where(half_lane >= EDGE * seg, y, packed[group, f, par])
                packed[group, f, par] = y
    for (group, f, par), y in packed.items():
        strip_ref[group, f, par] = y
    spare, back = spare_lanes(1 - core)
    for f in range(2):
        for par in range(2):
            first, second = packed[0, f, par], packed[1, f, par]
            corner_ref[f, par] = jnp.where(spare, pltpu.roll(second, back, 1), first)


def prep(place, right, scale, rows):
    vmem = pl.BlockSpec(memory_space=pltpu.VMEM)
    return pl.pallas_call(
        prep_kernel,
        out_shape=(tiles_of(rows, 2, 2), tiles_of(rows // SEGS, 2, 2), tiles_of(DEPTH, 2, 2), tiles_of(2, 2)),
        in_specs=[pl.BlockSpec(memory_space=pltpu.SMEM)] + [vmem] * 2,
        out_specs=(vmem,) * 4,
        compiler_params=pltpu.CompilerParams(vmem_limit_bytes=8 * MIB),
        name="prep",
    )(place, right, scale)


def pack_kernel(place_ref, own_ref, strip_ref, near_corner_ref, far_corner_ref, far_ref):
    rows = own_ref.shape[0]
    spare, back = spare_lanes(place_ref[0] % 2)
    for f in range(2):
        for par in range(2):
            for dist in range(1, DEPTH + 1):
                far_ref[dist - 1, f, par] = own_ref[rows - dist, f, par]
            first, second = strip_ref[0, f, par], strip_ref[1, f, par]
            far_corner_ref[f, par] = jnp.where(spare, pltpu.roll(first, back, 1), second)


def pack(place, own, strip, corner):
    vmem = pl.BlockSpec(memory_space=pltpu.VMEM)
    return pl.pallas_call(
        pack_kernel,
        out_shape=(tiles_of(2, 2), tiles_of(DEPTH, 2, 2)),
        in_specs=[pl.BlockSpec(memory_space=pltpu.SMEM)] + [vmem] * 3,
        out_specs=(vmem,) * 2,
        compiler_params=pltpu.CompilerParams(vmem_limit_bytes=8 * MIB),
        cost_estimate=pl.CostEstimate(flops=20000000, bytes_accessed=16 * MIB, transcendentals=0),
        name="pack",
    )(place, own, strip, corner)


def tiles_of(*n):
    return jax.ShapeDtypeStruct(n + (SUB, LANES), jnp.float32)


def conduct(x, y, factor):
    return jnp.where(jnp.minimum(x, y) > 0.0, (x + y) * (factor / HALF), 0.0)


def north(x):
    return pltpu.roll(x, LANES - 1, 1)


def south(x):
    return pltpu.roll(x, 1, 1)


def up(x):
    return pltpu.roll(x, SUB - 1, 0)


def down(x):
    return pltpu.roll(x, 1, 0)


class Lanes:
    def __init__(self, core):
        sub, lane = iotas()
        self.core = core
        self.base = WIDE + core * (WIDE - EDGE)
        self.left = lane < WIDE
        self.in_even = (lane >= self.base) & (lane < self.base + EDGE)
        self.in_odd = (lane >= self.base - WIDE) & (lane < self.base - WIDE + EDGE)

    def split(self, near, far, slot, spare=False):
        if far is None:
            even, odd = jnp.where(self.left, near, 0.0), jnp.where(self.left, 0.0, near)
        else:
            shift = self.base + (LANES - EDGE * slot)
            if spare:
                shift = shift + (LANES - (EDGE - SPARE)) + 2 * self.core * (EDGE - SPARE)
            far = pltpu.roll(far, lax.rem(shift, LANES), 1)
            even = jnp.where(self.left, near, jnp.where(self.in_even, far, 0.0))
            odd = jnp.where(self.left, jnp.where(self.in_odd, far, 0.0), near)
        return even, pltpu.roll(odd, WIDE, 1)

    def tiles(self, ref, row, far_of, slot, spare, f):
        e0, o0 = self.split(ref[row, f, 0], far_of(f, 0), slot, spare)
        e1, o1 = self.split(ref[row, f, 1], far_of(f, 1), slot, spare)
        return [e0, e1, o0, o1]

    def own(self, ref, strip_ref, r, f):
        group, slot = divmod(r, SEGS)
        return self.tiles(ref, r, lambda f, par: strip_ref[group, f, par], slot, False, f)

    def beyond(self, ref, corner, dist, f, near):
        slot = (dist - 1) % SEGS
        if not near:
            slot = SEGS - 1 - slot
        far = corner if dist < DEPTH else (lambda f, par: None)
        return self.tiles(ref, dist - 1, far, slot, dist > SEGS, f)


def row_coefs(w):
    sub, _ = iotas()
    out = {name: [None] * n for name, n in TILES.items() if name != "ce"}
    lat = [None] * 4
    for par in range(2):
        even, odd = w[par], w[2 + par]
        out["cl"][par] = conduct(even, odd, 0.5)
        lat[2 + par] = conduct(odd, north(even), 0.5)
        lat[par] = south(lat[2 + par])
    out["cn"] = list(lat)
    for side in range(2):
        even, odd = w[2 * side], w[2 * side + 1]
        out["ca"][side] = conduct(even, odd, 0.5 * vert_ratio)
        above = jnp.where(sub == SUB - 1, 0.0, up(even))
        cb = conduct(odd, above, 0.5 * vert_ratio)
        out["cb"][2 * side : 2 * side + 2] = [down(cb), cb]
    for t in range(4):
        hw = w[t] * (helm_shift / HALF) + (lat[t] + out["cb"][t])
        out["hw"][t] = hw
        out["d0"][t] = MU - hw
        out["d1"][t] = 2.0 * MU - hw
    return out


def sweep(span, step, read, write, coef):
    turn, stage = divmod(step - 1, EVERY)
    first = span[0]
    before, now = read(step - 1, first - 1), read(step - 1, first)
    last_flux = [coef("ce", first - 1, t) * (now[t] - before[t]) for t in range(4)]
    for r in span:
        ahead = read(step - 1, r + 1)
        flux = [coef("ce", r, t) * (ahead[t] - now[t]) for t in range(4)]
        acc = [flux[t] - last_flux[t] for t in range(4)]
        for par in range(2):
            even, odd = now[par], now[2 + par]
            fl = coef("cl", r, par) * (odd - even)
            acc[par] = acc[par] + (coef("cn", r, par) * south(odd) + fl)
            acc[2 + par] = acc[2 + par] + (coef("cn", r, 2 + par) * north(even) - fl)
        for s in range(2):
            even, odd = now[2 * s], now[2 * s + 1]
            fa = coef("ca", r, s) * (odd - even)
            acc[2 * s] = acc[2 * s] + (coef("cb", r, 2 * s) * down(odd) + fa)
            acc[2 * s + 1] = acc[2 * s + 1] + (coef("cb", r, 2 * s + 1) * up(even) - fa)
        v = read(turn * EVERY, r) if stage else None
        out = []
        for t in range(4):
            if stage == 0:
                y = acc[t] + coef("d1", r, t) * now[t]
            elif stage < CHEB:
                y = acc[t] + coef("d0", r, t) * now[t] + (NU if stage == 1 else MU * NU) * v[t]
            else:
                y = v[t] - STEP * (coef("hw", r, t) * now[t] - acc[t])
            out.append(y)
        write(step, r, out)
        now, last_flux = ahead, flux


class Moments:
    def __init__(self):
        self.acc = [[None] * 4 for _ in range(2 * ITERS)]

    def add(self, j, x, y):
        for t in range(4):
            term = x[t] * y[t]
            self.acc[j][t] = term if self.acc[j][t] is None else self.acc[j][t] + term

    def step(self, step, r, tiles, read):
        turn, stage = divmod(step - 1, EVERY)
        if stage == CHEB - 1:
            self.add(2 * turn, tiles, read(turn * EVERY, r))
        elif stage == CHEB:
            self.add(2 * turn + 1, tiles, read(step - 1, r))

    def total(self, j):
        a, b, c, d = self.acc[j]
        return (a + b) + (c + d)


def first_u(rows, k):
    return rows - (k * EVERY + CHEB), rows - (k + 1) * EVERY


def near_kernel(place_ref, own_ref, near_ref, corner_ref, strip_ref, *refs):
    rows = own_ref.shape[0]
    edge_ref, kept_ref, u_ref, r_ref, part_ref = refs[:5]
    coef_refs = dict(zip(NAMES, refs[5:13]))
    w_ref, v_ref, p_ref, q_ref = refs[13:]
    lanes = Lanes(place_ref[0] % 2)
    bufs = (v_ref, p_ref, q_ref, p_ref)

    def read(step, r):
        return [bufs[step % EVERY][r + DEPTH, t] for t in range(4)]

    def coef(name, r, t):
        return coef_refs[name][r + DEPTH, t]

    sums = Moments()

    def write(step, r, tiles):
        spread(bufs[step % EVERY], (r + DEPTH,), tiles)

    def keep(step):
        turn, stage = divmod(step - 1, EVERY)
        first = max(rows - EVERY - step, -DEPTH + step)
        for r in range(first, rows - step):
            tiles = read(step, r)
            if r >= rows - 2 - step:
                spread(edge_ref, (step, r - (rows - 2 - step)), tiles)
            if step % EVERY == 0:
                spread(kept_ref, (step // EVERY, r - (rows - EVERY - step)), tiles)

    for f, ref in enumerate((w_ref, v_ref)):
        for r in range(-DEPTH, rows):
            if r < 0:
                tiles = lanes.beyond(near_ref, lambda f, par: corner_ref[f, par], -r, f, True)
            else:
                tiles = lanes.own(own_ref, strip_ref, r, f)
            spread(ref, (r + DEPTH,), tiles)
    fill_coefs(coef_refs, w_ref)
    keep(0)
    for step in range(1, DEPTH + 1):
        turn, stage = divmod(step - 1, EVERY)
        sweep(range(step - DEPTH, rows - step), step, read, write, coef)
        if step < DEPTH:
            keep(step)
        for r in range(rows - step):
            tiles = read(step, r)
            if stage == CHEB - 1:
                spread(u_ref, (turn, r), tiles)
            elif stage == CHEB:
                spread(r_ref, (turn, r), tiles)
            sums.step(step, r, tiles, read)
    for j in range(2 * ITERS):
        part_ref[j] = sums.total(j)


def fill_coefs(coef_refs, w_ref):
    total = w_ref.shape[0]
    for k in range(total):
        w = [w_ref[k, t] for t in range(4)]
        for name, tiles in row_coefs(w).items():
            spread(coef_refs[name], (k,), tiles)
        if k < total - 1:
            spread(coef_refs["ce"], (k,), [conduct(w[t], w_ref[k + 1, t], 0.5) for t in range(4)])


def coef_scratch(total):
    return [pltpu.VMEM((total, TILES[name], SUB, LANES), jnp.float32) for name in NAMES]


def near_side(place, own, near, corner, strip):
    rows = own.shape[0]
    vmem = pl.BlockSpec(memory_space=pltpu.VMEM)
    outs = [tiles_of(DEPTH, 2, 4), tiles_of(ITERS, EVERY, 4)]
    outs += [tiles_of(ITERS, rows, 4)] * 2 + [tiles_of(2 * ITERS)]
    full = [pltpu.VMEM((rows + DEPTH, 4, SUB, LANES), jnp.float32)] * 4
    return pl.pallas_call(
        near_kernel,
        out_shape=outs,
        in_specs=[pl.BlockSpec(memory_space=pltpu.SMEM)] + [vmem] * 4,
        out_specs=[vmem] * len(outs),
        scratch_shapes=coef_scratch(rows + DEPTH) + full,
        compiler_params=pltpu.CompilerParams(vmem_limit_bytes=16 * MIB),
        cost_estimate=pl.CostEstimate(flops=20000000, bytes_accessed=4 * MIB, transcendentals=0),
        name="near_side",
    )(place, own, near, corner, strip)


def far_kernel(place_ref, own_ref, far_ref, corner_ref, strip_ref, edge_ref, kept_ref, part_in_ref, *refs):
    u_ref, r_ref, part_ref = refs[:3]
    coef_refs = dict(zip(NAMES, refs[3:11]))
    w_ref, v_ref, p_ref, q_ref = refs[11:]
    rows = own_ref.shape[0]
    base = rows - DEPTH - 1
    lanes = Lanes(place_ref[0] % 2)
    sub, lane = iotas()
    bufs = (v_ref, p_ref, q_ref, p_ref)

    def read(step, r):
        if r >= rows - step:
            return [bufs[step % EVERY][r, t] for t in range(4)]
        if r >= rows - 2 - step:
            return [edge_ref[step, r - (rows - 2 - step), t] for t in range(4)]
        return [kept_ref[step // EVERY, r - (rows - EVERY - step), t] for t in range(4)]

    def coef(name, r, t):
        return coef_refs[name][r - base, t]

    sums = Moments()

    def write(step, r, tiles):
        spread(bufs[step % EVERY], (r,), tiles)

    for r in range(base, rows + DEPTH):
        if r < rows:
            w = lanes.own(own_ref, strip_ref, r, 0)
        else:
            w, v = (
                lanes.beyond(far_ref, lambda f, par: corner_ref[f, par], r - rows + 1, f, False) for f in range(2)
            )
            spread(v_ref, (r,), v)
        spread(w_ref, (r - base,), w)
    fill_coefs(coef_refs, w_ref)
    for step in range(1, DEPTH + 1):
        turn, stage = divmod(step - 1, EVERY)
        sweep(range(rows - step, rows + DEPTH - step), step, read, write, coef)
        for r in range(rows - step, rows):
            tiles = read(step, r)
            if stage == CHEB - 1:
                spread(u_ref, (turn, r), tiles)
            elif stage == CHEB:
                spread(r_ref, (turn, r), tiles)
            sums.step(step, r, tiles, read)
    block = jnp.zeros((SUB, LANES), jnp.float32)
    for j in range(2 * ITERS):
        part = jnp.where(lanes.left, sums.total(j) + part_in_ref[j], 0.0)
        block = jnp.where(sub == j, jnp.sum(part, axis=0, keepdims=True), block)
    block = jnp.broadcast_to(jnp.sum(block, axis=1, keepdims=True), (SUB, LANES))
    row = jnp.sum(jnp.where(sub == lane, block, 0.0), axis=0, keepdims=True)
    row = jnp.broadcast_to(row, (SUB, LANES))
    for n in range(0, part_ref.shape[0], SUB):
        part_ref[n : n + SUB, :] = row


def far_side(place, own, far, corner, strip, edge, kept, part, peers):
    rows = own.shape[0]
    vmem = pl.BlockSpec(memory_space=pltpu.VMEM)
    outs = [tiles_of(ITERS, rows, 4)] * 2 + [jax.ShapeDtypeStruct((peers, LANES), jnp.float32)]
    full = [pltpu.VMEM((2 * DEPTH + 1, 4, SUB, LANES), jnp.float32)]
    full += [pltpu.VMEM((rows + DEPTH, 4, SUB, LANES), jnp.float32)] * 3
    return pl.pallas_call(
        far_kernel,
        out_shape=outs,
        in_specs=[pl.BlockSpec(memory_space=pltpu.SMEM)] + [vmem] * 7,
        out_specs=[vmem] * 3,
        scratch_shapes=coef_scratch(2 * DEPTH + 1) + full,
        compiler_params=pltpu.CompilerParams(vmem_limit_bytes=16 * MIB),
        cost_estimate=pl.CostEstimate(flops=15000000, bytes_accessed=4 * MIB, transcendentals=0),
        name="far_side",
    )(place, own, far, corner, strip, edge, kept, part)


def times_t(poly):
    out = [poly[0]]
    for i in range(1, len(poly)):
        out.append(poly[i] - poly[i - 1])
    out.append(-poly[-1])
    return out


def add_scaled(left, factor, right):
    out = []
    for i in range(max(len(left), len(right))):
        if i >= len(right):
            out.append(left[i])
        elif i >= len(left):
            out.append(factor * right[i])
        else:
            out.append(left[i] + factor * right[i])
    return out


def inner(left, right, moments):
    total = None
    for i, x in enumerate(left):
        for j, y in enumerate(right):
            term = x * y * moments[i + j]
            total = term if total is None else total + term
    return total


def last_kernel(place_ref, sums_ref, own_ref, u_near_ref, r_near_ref, u_far_ref, r_far_ref, sol_ref, res_ref):
    rows = own_ref.shape[0]
    flip = place_ref[0] // 2
    acc = sums_ref[:SUB, :]
    for n in range(SUB, sums_ref.shape[0], SUB):
        acc = acc + sums_ref[n : n + SUB, :]
    acc = jnp.sum(acc, axis=0, keepdims=True)
    moments = [jnp.broadcast_to(acc[:, j : j + 1], (SUB, LANES)) for j in range(2 * ITERS)]
    res = [jnp.ones((SUB, LANES), jnp.float32)]
    direction = res
    sol = None
    gamma = alpha = None
    for turn in range(ITERS):
        gamma_now = inner(res, res, moments)
        delta = inner(times_t(res), res, moments)
        if turn == 0:
            alpha = gamma_now / delta
            sol = [alpha]
        else:
            beta = gamma_now / gamma
            alpha = gamma_now / (delta - beta * gamma_now / alpha)
            direction = add_scaled(res, beta, direction)
            sol = add_scaled(sol, alpha, direction)
        res = add_scaled(res, -alpha, times_t(direction))
        gamma = gamma_now
    sol = [x * (STEP / HALF) for x in sol]
    _, lane = iotas()
    left = lane < WIDE
    mixed = WIDE * (lane % 2) + lane // 2
    for i in range(rows):
        u_refs, r_refs = [], []
        for k in range(ITERS):
            n_u, n_r = first_u(rows, k)
            u_refs.append(u_near_ref if i < n_u else u_far_ref)
            r_refs.append(r_near_ref if i < n_r else r_far_ref)
        for par in range(2):
            at = pl.ds(par * rows + column(rows, i, flip), SUB, stride=2 * rows)
            pair = []
            for t in (par, 2 + par):
                x = sol[0] * u_refs[0][0, i, t]
                y = res[1] * r_refs[0][0, i, t]
                for k in range(1, ITERS):
                    x = x + sol[k] * u_refs[k][k, i, t]
                    y = y + res[k + 1] * r_refs[k][k, i, t]
                pair.append((x, y))
            x, y = (jnp.where(left, even, pltpu.roll(odd, WIDE, 1)) for even, odd in zip(*pair))
            x = take_lanes(x, mixed)
            y = take_lanes(y + res[0] * own_ref[i, 1, par], mixed)
            sol_ref[at, :] = x
            res_ref[at, :] = y


def last(place, sums, own, *vectors):
    rows = own.shape[0]
    vmem = pl.BlockSpec(memory_space=pltpu.VMEM)
    out = jax.ShapeDtypeStruct((2 * SUB * rows, LANES), jnp.float32)
    return pl.pallas_call(
        last_kernel,
        out_shape=(out, out),
        in_specs=[pl.BlockSpec(memory_space=pltpu.SMEM)] + [vmem] * (2 + len(vectors)),
        out_specs=(vmem,) * 2,
        compiler_params=pltpu.CompilerParams(vmem_limit_bytes=48 * MIB),
        name="combine",
    )(place, sums, own, *vectors)


def local(right_side, scale, land_mask, bottom):
    levels, rows, lats = right_side.shape
    lon = lax.axis_size("lon")
    lat = lax.axis_size("lat")
    peers = lon * lat
    assert levels == 2 * SUB and lats == LANES and lat == 2
    assert rows == 2 * SEGS and rows >= DEPTH and 2 * EDGE >= DEPTH
    assert lon % 2 == 0 and peers % SUB == 0
    both = ("lon", "lat")

    def links(to):
        return [(i * lat + j, to(i, j)[0] % lon * lat + to(i, j)[1]) for i in range(lon) for j in range(lat)]

    beyond = lambda i: i + 1 if i % 2 else i - 1
    place = lax.axis_index("lat") + 2 * (1 - lax.axis_index("lon") % 2)
    place = place.astype(jnp.int32).reshape(1)
    depth = lax.broadcasted_iota(jnp.int32, right_side.shape, 0)
    wet = depth < jnp.where(land_mask == 1, bottom, 0)[None]
    right, weight = (jnp.where(wet, x, 0.0).reshape(levels * rows, lats) for x in (right_side, scale))
    own, strip, near, corner = prep(place, right, weight, rows)
    corner = lax.ppermute(corner, both, links(lambda i, j: (i ^ 1, 1 - j)))
    near = lax.ppermute(near, both, links(lambda i, j: (i ^ 1, j)))
    strip = lax.ppermute(strip, both, links(lambda i, j: (i, 1 - j)))
    far_corner, far = pack(place, own, strip, corner)
    far = lax.ppermute(far, both, links(lambda i, j: (beyond(i), j)))
    far_corner = lax.ppermute(far_corner, both, links(lambda i, j: (beyond(i), j)))
    edge, kept, u_near, r_near, part = near_side(place, own, near, corner, strip)
    u_far, r_far, parts = far_side(place, own, far, far_corner, strip, edge, kept, part, peers)
    sums = lax.all_to_all(parts, both, 0, 0, tiled=True)
    sol, res = last(place, sums, own, u_near, r_near, u_far, r_far)
    return sol.reshape(right_side.shape), res.reshape(right_side.shape)


def solution(mesh):
    field = P("member", "lon", "lat")
    mask = P(("member", "lon"), "lat")
    return jax.shard_map(
        local,
        mesh=mesh,
        in_specs=(field, field, mask, mask),
        out_specs=(field, field),
        check_vma=False,
    )
```

```python
import functools

import jax
import jax.numpy as jnp
from jax import lax
from jax.experimental import pallas as pl
from jax.experimental.pallas import tpu as pltpu
from jax.sharding import PartitionSpec as P

ITERS = 3
CHEB = 3
DEPTH = ITERS * (CHEB + 1)
SUB = 8
LANES = 128
WIDE = LANES // 2
SEGS = 8
EDGE = WIDE // SEGS

helm_shift = 0.05
vert_ratio = 4.0
cheb_low = 4.0
cheb_high = 150.0

CENTRE = 0.5 * (cheb_high + cheb_low)
HALF = 0.5 * (cheb_high - cheb_low)
MU = CENTRE / HALF
NU = MU * MU - 1.0
STEP = 5.0
NAMES = ("ce", "cn", "cl", "ca", "cb", "d1", "d0", "hw")
TILES = dict(ce=4, cn=4, cl=2, ca=2, cb=4, d1=4, d0=4, hw=4)
EVERY = CHEB + 1
SPARE = 2
MIB = 1024 * 1024


def take_lanes(x, index):
    return jnp.take_along_axis(x, index, axis=1, mode="promise_in_bounds")


def spread(ref, index, tiles):
    for t, tile in enumerate(tiles):
        ref[index + (t,)] = tile


def iotas():
    sub = lax.broadcasted_iota(jnp.int32, (SUB, LANES), 0)
    lane = lax.broadcasted_iota(jnp.int32, (SUB, LANES), 1)
    return sub, lane


def column(rows, r, flip):
    return r + flip * (rows - 1 - 2 * r)


def spare_lanes(core):
    _, lane = iotas()
    back = lax.rem(EDGE - SPARE + core * (LANES - 2 * (EDGE - SPARE)), LANES)
    start = (1 - core) * (EDGE - SPARE)
    in_slot = lane % EDGE
    return (in_slot >= start) & (in_slot < start + SPARE), back


def prep_kernel(place_ref, both_ref, land_ref, bottom_ref, own_ref, strip_ref, near_ref, corner_ref):
    rows = own_ref.shape[0]
    core, flip = place_ref[0] % 2, place_ref[0] // 2
    sub, lane = iotas()
    half_lane = lane % WIDE
    apart = 2 * half_lane + lane // WIDE
    packed = {}
    for r in range(rows):
        group, seg = divmod(r, SEGS)
        shift = lax.rem(EDGE * seg + (1 - core) * (WIDE + EDGE), LANES)
        i = column(rows, r, flip)
        deep = jnp.where(land_ref[pl.ds(i, 1), :] == 1, bottom_ref[pl.ds(i, 1), :], 0)
        deep = jnp.broadcast_to(deep, (SUB, LANES))
        for par in range(2):
            wet = 2 * sub + par < deep
            for f in range(2):
                at = pl.ds((2 * SUB * f + par) * rows + i, SUB, stride=2 * rows)
                x = take_lanes(jnp.where(wet, both_ref[at, :], 0.0), apart)
                own_ref[r, f, par] = x
                if r < DEPTH:
                    near_ref[r, f, par] = x
                y = pltpu.roll(x, shift, 1)
                if seg:
                    y = jnp.where(half_lane >= EDGE * seg, y, packed[group, f, par])
                packed[group, f, par] = y
    for (group, f, par), y in packed.items():
        strip_ref[group, f, par] = y
    spare, back = spare_lanes(1 - core)
    for f in range(2):
        for par in range(2):
            first, second = packed[0, f, par], packed[1, f, par]
            corner_ref[f, par] = jnp.where(spare, pltpu.roll(second, back, 1), first)


def prep(place, fields, land, bottom):
    rows = land.shape[0]
    vmem = pl.BlockSpec(memory_space=pltpu.VMEM)
    return pl.pallas_call(
        prep_kernel,
        out_shape=(tiles_of(rows, 2, 2), tiles_of(rows // SEGS, 2, 2), tiles_of(DEPTH, 2, 2), tiles_of(2, 2)),
        in_specs=[pl.BlockSpec(memory_space=pltpu.SMEM)] + [vmem] * 3,
        out_specs=(vmem,) * 4,
        compiler_params=pltpu.CompilerParams(vmem_limit_bytes=8 * MIB),
        name="prep",
    )(place, fields, land, bottom)


def pack_kernel(place_ref, own_ref, strip_ref, near_corner_ref, far_corner_ref, far_ref):
    rows = own_ref.shape[0]
    spare, back = spare_lanes(place_ref[0] % 2)
    for f in range(2):
        for par in range(2):
            for dist in range(1, DEPTH + 1):
                far_ref[dist - 1, f, par] = own_ref[rows - dist, f, par]
            first, second = strip_ref[0, f, par], strip_ref[1, f, par]
            far_corner_ref[f, par] = jnp.where(spare, pltpu.roll(first, back, 1), second)


def pack(place, own, strip, corner):
    vmem = pl.BlockSpec(memory_space=pltpu.VMEM)
    return pl.pallas_call(
        pack_kernel,
        out_shape=(tiles_of(2, 2), tiles_of(DEPTH, 2, 2)),
        in_specs=[pl.BlockSpec(memory_space=pltpu.SMEM)] + [vmem] * 3,
        out_specs=(vmem,) * 2,
        compiler_params=pltpu.CompilerParams(vmem_limit_bytes=8 * MIB),
        cost_estimate=pl.CostEstimate(flops=20000000, bytes_accessed=16 * MIB, transcendentals=0),
        name="pack",
    )(place, own, strip, corner)


def tiles_of(*n):
    return jax.ShapeDtypeStruct(n + (SUB, LANES), jnp.float32)


def conduct(x, y, factor):
    return jnp.where(jnp.minimum(x, y) > 0.0, (x + y) * (factor / HALF), 0.0)


def north(x):
    return pltpu.roll(x, LANES - 1, 1)


def south(x):
    return pltpu.roll(x, 1, 1)


def up(x):
    return pltpu.roll(x, SUB - 1, 0)


def down(x):
    return pltpu.roll(x, 1, 0)


class Lanes:
    def __init__(self, core):
        sub, lane = iotas()
        self.core = core
        self.base = WIDE + core * (WIDE - EDGE)
        self.left = lane < WIDE
        self.in_even = (lane >= self.base) & (lane < self.base + EDGE)
        self.in_odd = (lane >= self.base - WIDE) & (lane < self.base - WIDE + EDGE)

    def split(self, near, far, slot, spare=False):
        if far is None:
            even, odd = jnp.where(self.left, near, 0.0), jnp.where(self.left, 0.0, near)
        else:
            shift = self.base + (LANES - EDGE * slot)
            if spare:
                shift = shift + (LANES - (EDGE - SPARE)) + 2 * self.core * (EDGE - SPARE)
            far = pltpu.roll(far, lax.rem(shift, LANES), 1)
            even = jnp.where(self.left, near, jnp.where(self.in_even, far, 0.0))
            odd = jnp.where(self.left, jnp.where(self.in_odd, far, 0.0), near)
        return even, pltpu.roll(odd, WIDE, 1)

    def tiles(self, ref, row, far_of, slot, spare, f):
        e0, o0 = self.split(ref[row, f, 0], far_of(f, 0), slot, spare)
        e1, o1 = self.split(ref[row, f, 1], far_of(f, 1), slot, spare)
        return [e0, e1, o0, o1]

    def own(self, ref, strip_ref, r, f):
        group, slot = divmod(r, SEGS)
        return self.tiles(ref, r, lambda f, par: strip_ref[group, f, par], slot, False, f)

    def beyond(self, ref, corner, dist, f, near):
        slot = (dist - 1) % SEGS
        if not near:
            slot = SEGS - 1 - slot
        far = corner if dist < DEPTH else (lambda f, par: None)
        return self.tiles(ref, dist - 1, far, slot, dist > SEGS, f)


def row_coefs(w):
    sub, _ = iotas()
    out = {name: [None] * n for name, n in TILES.items() if name != "ce"}
    lat = [None] * 4
    for par in range(2):
        even, odd = w[par], w[2 + par]
        out["cl"][par] = conduct(even, odd, 0.5)
        lat[2 + par] = conduct(odd, north(even), 0.5)
        lat[par] = south(lat[2 + par])
    out["cn"] = list(lat)
    for side in range(2):
        even, odd = w[2 * side], w[2 * side + 1]
        out["ca"][side] = conduct(even, odd, 0.5 * vert_ratio)
        above = jnp.where(sub == SUB - 1, 0.0, up(even))
        cb = conduct(odd, above, 0.5 * vert_ratio)
        out["cb"][2 * side : 2 * side + 2] = [down(cb), cb]
    for t in range(4):
        hw = w[t] * (helm_shift / HALF) + (lat[t] + out["cb"][t])
        out["hw"][t] = hw
        out["d0"][t] = MU - hw
        out["d1"][t] = 2.0 * MU - hw
    return out


def sweep(span, step, read, write, coef):
    turn, stage = divmod(step - 1, EVERY)
    first = span[0]
    before, now = read(step - 1, first - 1), read(step - 1, first)
    last_flux = [coef("ce", first - 1, t) * (now[t] - before[t]) for t in range(4)]
    for r in span:
        ahead = read(step - 1, r + 1)
        flux = [coef("ce", r, t) * (ahead[t] - now[t]) for t in range(4)]
        acc = [flux[t] - last_flux[t] for t in range(4)]
        for par in range(2):
            even, odd = now[par], now[2 + par]
            fl = coef("cl", r, par) * (odd - even)
            acc[par] = acc[par] + (coef("cn", r, par) * south(odd) + fl)
            acc[2 + par] = acc[2 + par] + (coef("cn", r, 2 + par) * north(even) - fl)
        for s in range(2):
            even, odd = now[2 * s], now[2 * s + 1]
            fa = coef("ca", r, s) * (odd - even)
            acc[2 * s] = acc[2 * s] + (coef("cb", r, 2 * s) * down(odd) + fa)
            acc[2 * s + 1] = acc[2 * s + 1] + (coef("cb", r, 2 * s + 1) * up(even) - fa)
        v = read(turn * EVERY, r) if stage else None
        out = []
        for t in range(4):
            if stage == 0:
                y = acc[t] + coef("d1", r, t) * now[t]
            elif stage < CHEB:
                y = acc[t] + coef("d0", r, t) * now[t] + (NU if stage == 1 else MU * NU) * v[t]
            else:
                y = v[t] - STEP * (coef("hw", r, t) * now[t] - acc[t])
            out.append(y)
        write(step, r, out)
        now, last_flux = ahead, flux


class Moments:
    def __init__(self):
        self.acc = [[None] * 4 for _ in range(2 * ITERS)]

    def add(self, j, x, y):
        for t in range(4):
            term = x[t] * y[t]
            self.acc[j][t] = term if self.acc[j][t] is None else self.acc[j][t] + term

    def step(self, step, r, tiles, read):
        turn, stage = divmod(step - 1, EVERY)
        if stage == CHEB - 1:
            self.add(2 * turn, tiles, read(turn * EVERY, r))
        elif stage == CHEB:
            self.add(2 * turn + 1, tiles, read(step - 1, r))

    def total(self, j):
        a, b, c, d = self.acc[j]
        return (a + b) + (c + d)


def first_u(rows, k):
    return rows - (k * EVERY + CHEB), rows - (k + 1) * EVERY


def near_kernel(place_ref, own_ref, near_ref, corner_ref, strip_ref, *refs):
    rows = own_ref.shape[0]
    edge_ref, kept_ref, u_ref, r_ref, part_ref = refs[:5]
    coef_refs = dict(zip(NAMES, refs[5:13]))
    w_ref, v_ref, p_ref, q_ref = refs[13:]
    lanes = Lanes(place_ref[0] % 2)
    bufs = (v_ref, p_ref, q_ref, p_ref)

    def read(step, r):
        return [bufs[step % EVERY][r + DEPTH, t] for t in range(4)]

    def coef(name, r, t):
        return coef_refs[name][r + DEPTH, t]

    sums = Moments()

    def write(step, r, tiles):
        spread(bufs[step % EVERY], (r + DEPTH,), tiles)

    def keep(step):
        turn, stage = divmod(step - 1, EVERY)
        first = max(rows - EVERY - step, -DEPTH + step)
        for r in range(first, rows - step):
            tiles = read(step, r)
            if r >= rows - 2 - step:
                spread(edge_ref, (step, r - (rows - 2 - step)), tiles)
            if step % EVERY == 0:
                spread(kept_ref, (step // EVERY, r - (rows - EVERY - step)), tiles)

    for f, ref in enumerate((w_ref, v_ref)):
        for r in range(-DEPTH, rows):
            if r < 0:
                tiles = lanes.beyond(near_ref, lambda f, par: corner_ref[f, par], -r, f, True)
            else:
                tiles = lanes.own(own_ref, strip_ref, r, f)
            spread(ref, (r + DEPTH,), tiles)
    fill_coefs(coef_refs, w_ref)
    keep(0)
    for step in range(1, DEPTH + 1):
        turn, stage = divmod(step - 1, EVERY)
        sweep(range(step - DEPTH, rows - step), step, read, write, coef)
        if step < DEPTH:
            keep(step)
        for r in range(rows - step):
            tiles = read(step, r)
            if stage == CHEB - 1:
                spread(u_ref, (turn, r), tiles)
            elif stage == CHEB:
                spread(r_ref, (turn, r), tiles)
            sums.step(step, r, tiles, read)
    for j in range(2 * ITERS):
        part_ref[j] = sums.total(j)


def fill_coefs(coef_refs, w_ref):
    total = w_ref.shape[0]
    for k in range(total):
        w = [w_ref[k, t] for t in range(4)]
        for name, tiles in row_coefs(w).items():
            spread(coef_refs[name], (k,), tiles)
        if k < total - 1:
            spread(coef_refs["ce"], (k,), [conduct(w[t], w_ref[k + 1, t], 0.5) for t in range(4)])


def coef_scratch(total):
    return [pltpu.VMEM((total, TILES[name], SUB, LANES), jnp.float32) for name in NAMES]


def near_side(place, own, near, corner, strip):
    rows = own.shape[0]
    vmem = pl.BlockSpec(memory_space=pltpu.VMEM)
    outs = [tiles_of(DEPTH, 2, 4), tiles_of(ITERS, EVERY, 4)]
    outs += [tiles_of(ITERS, rows, 4)] * 2 + [tiles_of(2 * ITERS)]
    full = [pltpu.VMEM((rows + DEPTH, 4, SUB, LANES), jnp.float32)] * 4
    return pl.pallas_call(
        near_kernel,
        out_shape=outs,
        in_specs=[pl.BlockSpec(memory_space=pltpu.SMEM)] + [vmem] * 4,
        out_specs=[vmem] * len(outs),
        scratch_shapes=coef_scratch(rows + DEPTH) + full,
        compiler_params=pltpu.CompilerParams(vmem_limit_bytes=16 * MIB),
        cost_estimate=pl.CostEstimate(flops=20000000, bytes_accessed=4 * MIB, transcendentals=0),
        name="near_side",
    )(place, own, near, corner, strip)


def far_kernel(place_ref, own_ref, far_ref, corner_ref, strip_ref, edge_ref, kept_ref, part_in_ref, *refs):
    u_ref, r_ref, part_ref = refs[:3]
    coef_refs = dict(zip(NAMES, refs[3:11]))
    w_ref, v_ref, p_ref, q_ref = refs[11:]
    rows = own_ref.shape[0]
    base = rows - DEPTH - 1
    lanes = Lanes(place_ref[0] % 2)
    sub, lane = iotas()
    bufs = (v_ref, p_ref, q_ref, p_ref)

    def read(step, r):
        if r >= rows - step:
            return [bufs[step % EVERY][r, t] for t in range(4)]
        if r >= rows - 2 - step:
            return [edge_ref[step, r - (rows - 2 - step), t] for t in range(4)]
        return [kept_ref[step // EVERY, r - (rows - EVERY - step), t] for t in range(4)]

    def coef(name, r, t):
        return coef_refs[name][r - base, t]

    sums = Moments()

    def write(step, r, tiles):
        spread(bufs[step % EVERY], (r,), tiles)

    for r in range(base, rows + DEPTH):
        if r < rows:
            w = lanes.own(own_ref, strip_ref, r, 0)
        else:
            w, v = (
                lanes.beyond(far_ref, lambda f, par: corner_ref[f, par], r - rows + 1, f, False) for f in range(2)
            )
            spread(v_ref, (r,), v)
        spread(w_ref, (r - base,), w)
    fill_coefs(coef_refs, w_ref)
    for step in range(1, DEPTH + 1):
        turn, stage = divmod(step - 1, EVERY)
        sweep(range(rows - step, rows + DEPTH - step), step, read, write, coef)
        for r in range(rows - step, rows):
            tiles = read(step, r)
            if stage == CHEB - 1:
                spread(u_ref, (turn, r), tiles)
            elif stage == CHEB:
                spread(r_ref, (turn, r), tiles)
            sums.step(step, r, tiles, read)
    block = jnp.zeros((SUB, LANES), jnp.float32)
    for j in range(2 * ITERS):
        part = jnp.where(lanes.left, sums.total(j) + part_in_ref[j], 0.0)
        block = jnp.where(sub == j, jnp.sum(part, axis=0, keepdims=True), block)
    block = jnp.broadcast_to(jnp.sum(block, axis=1, keepdims=True), (SUB, LANES))
    row = jnp.sum(jnp.where(sub == lane, block, 0.0), axis=0, keepdims=True)
    row = jnp.broadcast_to(row, (SUB, LANES))
    for n in range(0, part_ref.shape[0], SUB):
        part_ref[n : n + SUB, :] = row


def far_side(place, own, far, corner, strip, edge, kept, part, peers):
    rows = own.shape[0]
    vmem = pl.BlockSpec(memory_space=pltpu.VMEM)
    outs = [tiles_of(ITERS, rows, 4)] * 2 + [jax.ShapeDtypeStruct((peers, LANES), jnp.float32)]
    full = [pltpu.VMEM((2 * DEPTH + 1, 4, SUB, LANES), jnp.float32)]
    full += [pltpu.VMEM((rows + DEPTH, 4, SUB, LANES), jnp.float32)] * 3
    return pl.pallas_call(
        far_kernel,
        out_shape=outs,
        in_specs=[pl.BlockSpec(memory_space=pltpu.SMEM)] + [vmem] * 7,
        out_specs=[vmem] * 3,
        scratch_shapes=coef_scratch(2 * DEPTH + 1) + full,
        compiler_params=pltpu.CompilerParams(vmem_limit_bytes=16 * MIB),
        cost_estimate=pl.CostEstimate(flops=15000000, bytes_accessed=4 * MIB, transcendentals=0),
        name="far_side",
    )(place, own, far, corner, strip, edge, kept, part)


def times_t(poly):
    out = [poly[0]]
    for i in range(1, len(poly)):
        out.append(poly[i] - poly[i - 1])
    out.append(-poly[-1])
    return out


def add_scaled(left, factor, right):
    out = []
    for i in range(max(len(left), len(right))):
        if i >= len(right):
            out.append(left[i])
        elif i >= len(left):
            out.append(factor * right[i])
        else:
            out.append(left[i] + factor * right[i])
    return out


def inner(left, right, moments):
    total = None
    for i, x in enumerate(left):
        for j, y in enumerate(right):
            term = x * y * moments[i + j]
            total = term if total is None else total + term
    return total


def last_kernel(place_ref, sums_ref, own_ref, u_near_ref, r_near_ref, u_far_ref, r_far_ref, sol_ref, res_ref):
    rows = own_ref.shape[0]
    flip = place_ref[0] // 2
    acc = sums_ref[:SUB, :]
    for n in range(SUB, sums_ref.shape[0], SUB):
        acc = acc + sums_ref[n : n + SUB, :]
    acc = jnp.sum(acc, axis=0, keepdims=True)
    moments = [jnp.broadcast_to(acc[:, j : j + 1], (SUB, LANES)) for j in range(2 * ITERS)]
    res = [jnp.ones((SUB, LANES), jnp.float32)]
    direction = res
    sol = None
    gamma = alpha = None
    for turn in range(ITERS):
        gamma_now = inner(res, res, moments)
        delta = inner(times_t(res), res, moments)
        if turn == 0:
            alpha = gamma_now / delta
            sol = [alpha]
        else:
            beta = gamma_now / gamma
            alpha = gamma_now / (delta - beta * gamma_now / alpha)
            direction = add_scaled(res, beta, direction)
            sol = add_scaled(sol, alpha, direction)
        res = add_scaled(res, -alpha, times_t(direction))
        gamma = gamma_now
    sol = [x * (STEP / HALF) for x in sol]
    _, lane = iotas()
    left = lane < WIDE
    mixed = WIDE * (lane % 2) + lane // 2
    for i in range(rows):
        u_refs, r_refs = [], []
        for k in range(ITERS):
            n_u, n_r = first_u(rows, k)
            u_refs.append(u_near_ref if i < n_u else u_far_ref)
            r_refs.append(r_near_ref if i < n_r else r_far_ref)
        for par in range(2):
            at = pl.ds(par * rows + column(rows, i, flip), SUB, stride=2 * rows)
            pair = []
            for t in (par, 2 + par):
                x = sol[0] * u_refs[0][0, i, t]
                y = res[1] * r_refs[0][0, i, t]
                for k in range(1, ITERS):
                    x = x + sol[k] * u_refs[k][k, i, t]
                    y = y + res[k + 1] * r_refs[k][k, i, t]
                pair.append((x, y))
            x, y = (jnp.where(left, even, pltpu.roll(odd, WIDE, 1)) for even, odd in zip(*pair))
            x = take_lanes(x, mixed)
            y = take_lanes(y + res[0] * own_ref[i, 1, par], mixed)
            sol_ref[at, :] = x
            res_ref[at, :] = y


def last(place, sums, own, *vectors):
    rows = own.shape[0]
    vmem = pl.BlockSpec(memory_space=pltpu.VMEM)
    out = jax.ShapeDtypeStruct((2 * SUB * rows, LANES), jnp.float32)
    return pl.pallas_call(
        last_kernel,
        out_shape=(out, out),
        in_specs=[pl.BlockSpec(memory_space=pltpu.SMEM)] + [vmem] * (2 + len(vectors)),
        out_specs=(vmem,) * 2,
        compiler_params=pltpu.CompilerParams(vmem_limit_bytes=48 * MIB),
        name="combine",
    )(place, sums, own, *vectors)


def local(right_side, scale, land_mask, bottom):
    levels, rows, lats = right_side.shape
    lon = lax.axis_size("lon")
    lat = lax.axis_size("lat")
    peers = lon * lat
    assert levels == 2 * SUB and lats == LANES and lat == 2
    assert rows == 2 * SEGS and rows >= DEPTH and 2 * EDGE >= DEPTH
    assert lon % 2 == 0 and peers % SUB == 0
    both = ("lon", "lat")

    def links(to):
        return [(i * lat + j, to(i, j)[0] % lon * lat + to(i, j)[1]) for i in range(lon) for j in range(lat)]

    beyond = lambda i: i + 1 if i % 2 else i - 1
    place = lax.axis_index("lat") + 2 * (1 - lax.axis_index("lon") % 2)
    place = place.astype(jnp.int32).reshape(1)
    fields = jnp.stack([scale, right_side]).reshape(2 * levels * rows, lats)
    own, strip, near, corner = prep(place, fields, land_mask, bottom)
    corner = lax.ppermute(corner, both, links(lambda i, j: (i ^ 1, 1 - j)))
    near = lax.ppermute(near, both, links(lambda i, j: (i ^ 1, j)))
    strip = lax.ppermute(strip, both, links(lambda i, j: (i, 1 - j)))
    far_corner, far = pack(place, own, strip, corner)
    far = lax.ppermute(far, both, links(lambda i, j: (beyond(i), j)))
    far_corner = lax.ppermute(far_corner, both, links(lambda i, j: (beyond(i), j)))
    edge, kept, u_near, r_near, part = near_side(place, own, near, corner, strip)
    u_far, r_far, parts = far_side(place, own, far, far_corner, strip, edge, kept, part, peers)
    sums = lax.all_to_all(parts, both, 0, 0, tiled=True)
    sol, res = last(place, sums, own, u_near, r_near, u_far, r_far)
    return sol.reshape(right_side.shape), res.reshape(right_side.shape)


def solution(mesh):
    field = P("member", "lon", "lat")
    mask = P(("member", "lon"), "lat")
    return jax.shard_map(
        local,
        mesh=mesh,
        in_specs=(field, field, mask, mask),
        out_specs=(field, field),
        check_vma=False,
    )
```

```python
import functools

import jax
import jax.numpy as jnp
from jax import lax
from jax.experimental import pallas as pl
from jax.experimental.pallas import tpu as pltpu
from jax.sharding import PartitionSpec as P

ITERS = 3
CHEB = 3
DEPTH = ITERS * (CHEB + 1)
SUB = 8
LANES = 128
WIDE = LANES // 2
SEGS = 8
EDGE = WIDE // SEGS

helm_shift = 0.05
vert_ratio = 4.0
cheb_low = 4.0
cheb_high = 150.0

CENTRE = 0.5 * (cheb_high + cheb_low)
HALF = 0.5 * (cheb_high - cheb_low)
MU = CENTRE / HALF
NU = MU * MU - 1.0
STEP = 5.0
NAMES = ("ce", "cn", "cl", "ca", "cb", "d1", "d0", "hw")
TILES = dict(ce=4, cn=4, cl=2, ca=2, cb=4, d1=4, d0=4, hw=4)
EVERY = CHEB + 1
SPARE = 2
MIB = 1024 * 1024


def take_lanes(x, index):
    return jnp.take_along_axis(x, index, axis=1, mode="promise_in_bounds")


def spread(ref, index, tiles):
    for t, tile in enumerate(tiles):
        ref[index + (t,)] = tile


def iotas():
    sub = lax.broadcasted_iota(jnp.int32, (SUB, LANES), 0)
    lane = lax.broadcasted_iota(jnp.int32, (SUB, LANES), 1)
    return sub, lane


def column(rows, r, flip):
    return r + flip * (rows - 1 - 2 * r)


def spare_lanes(core):
    _, lane = iotas()
    back = lax.rem(EDGE - SPARE + core * (LANES - 2 * (EDGE - SPARE)), LANES)
    start = (1 - core) * (EDGE - SPARE)
    in_slot = lane % EDGE
    return (in_slot >= start) & (in_slot < start + SPARE), back


def prep_kernel(place_ref, both_ref, land_ref, bottom_ref, own_ref, strip_ref, near_ref, corner_ref):
    rows = own_ref.shape[0]
    core, flip = place_ref[0] % 2, place_ref[0] // 2
    sub, lane = iotas()
    half_lane = lane % WIDE
    apart = 2 * half_lane + lane // WIDE
    packed = {}
    for r in range(rows):
        group, seg = divmod(r, SEGS)
        shift = lax.rem(EDGE * seg + (1 - core) * (WIDE + EDGE), LANES)
        i = column(rows, r, flip)
        deep = jnp.where(land_ref[pl.ds(i, 1), :] == 1, bottom_ref[pl.ds(i, 1), :], 0)
        deep = jnp.broadcast_to(deep, (SUB, LANES))
        for par in range(2):
            wet = 2 * sub + par < deep
            for f in range(2):
                at = pl.ds((2 * SUB * f + par) * rows + i, SUB, stride=2 * rows)
                x = take_lanes(jnp.where(wet, both_ref[at, :], 0.0), apart)
                own_ref[r, f, par] = x
                if r < DEPTH:
                    near_ref[r, f, par] = x
                y = pltpu.roll(x, shift, 1)
                if seg:
                    y = jnp.where(half_lane >= EDGE * seg, y, packed[group, f, par])
                packed[group, f, par] = y
    for (group, f, par), y in packed.items():
        strip_ref[group, f, par] = y
    spare, back = spare_lanes(1 - core)
    for f in range(2):
        for par in range(2):
            first, second = packed[0, f, par], packed[1, f, par]
            corner_ref[f, par] = jnp.where(spare, pltpu.roll(second, back, 1), first)


def prep(place, fields, land, bottom):
    rows = land.shape[0]
    vmem = pl.BlockSpec(memory_space=pltpu.VMEM)
    return pl.pallas_call(
        prep_kernel,
        out_shape=(tiles_of(rows, 2, 2), tiles_of(rows // SEGS, 2, 2), tiles_of(DEPTH, 2, 2), tiles_of(2, 2)),
        in_specs=[pl.BlockSpec(memory_space=pltpu.SMEM)] + [vmem] * 3,
        out_specs=(vmem,) * 4,
        compiler_params=pltpu.CompilerParams(vmem_limit_bytes=8 * MIB),
        name="prep",
    )(place, fields, land, bottom)


def pack_kernel(place_ref, own_ref, strip_ref, near_corner_ref, far_corner_ref, far_ref, tile_ref):
    rows = own_ref.shape[0]
    spare, back = spare_lanes(place_ref[0] % 2)
    for f in range(2):
        for par in range(2):
            for dist in range(1, DEPTH + 1):
                far_ref[dist - 1, f, par] = own_ref[rows - dist, f, par]
            first, second = strip_ref[0, f, par], strip_ref[1, f, par]
            far_corner_ref[f, par] = jnp.where(spare, pltpu.roll(first, back, 1), second)
    lanes = Lanes(place_ref[0] % 2)
    for f in range(2):
        for r in range(rows):
            spread(tile_ref, (f, r), lanes.own(own_ref, strip_ref, r, f))


def pack(place, own, strip, corner):
    vmem = pl.BlockSpec(memory_space=pltpu.VMEM)
    return pl.pallas_call(
        pack_kernel,
        out_shape=(tiles_of(2, 2), tiles_of(DEPTH, 2, 2), tiles_of(2, own.shape[0], 4)),
        in_specs=[pl.BlockSpec(memory_space=pltpu.SMEM)] + [vmem] * 3,
        out_specs=(vmem,) * 3,
        compiler_params=pltpu.CompilerParams(vmem_limit_bytes=8 * MIB),
        cost_estimate=pl.CostEstimate(flops=20000000, bytes_accessed=16 * MIB, transcendentals=0),
        name="pack",
    )(place, own, strip, corner)


def tiles_of(*n):
    return jax.ShapeDtypeStruct(n + (SUB, LANES), jnp.float32)


def conduct(x, y, factor):
    return jnp.where(jnp.minimum(x, y) > 0.0, (x + y) * (factor / HALF), 0.0)


def north(x):
    return pltpu.roll(x, LANES - 1, 1)


def south(x):
    return pltpu.roll(x, 1, 1)


def up(x):
    return pltpu.roll(x, SUB - 1, 0)


def down(x):
    return pltpu.roll(x, 1, 0)


class Lanes:
    def __init__(self, core):
        sub, lane = iotas()
        self.core = core
        self.base = WIDE + core * (WIDE - EDGE)
        self.left = lane < WIDE
        self.in_even = (lane >= self.base) & (lane < self.base + EDGE)
        self.in_odd = (lane >= self.base - WIDE) & (lane < self.base - WIDE + EDGE)

    def split(self, near, far, slot, spare=False):
        if far is None:
            even, odd = jnp.where(self.left, near, 0.0), jnp.where(self.left, 0.0, near)
        else:
            shift = self.base + (LANES - EDGE * slot)
            if spare:
                shift = shift + (LANES - (EDGE - SPARE)) + 2 * self.core * (EDGE - SPARE)
            far = pltpu.roll(far, lax.rem(shift, LANES), 1)
            even = jnp.where(self.left, near, jnp.where(self.in_even, far, 0.0))
            odd = jnp.where(self.left, jnp.where(self.in_odd, far, 0.0), near)
        return even, pltpu.roll(odd, WIDE, 1)

    def tiles(self, ref, row, far_of, slot, spare, f):
        e0, o0 = self.split(ref[row, f, 0], far_of(f, 0), slot, spare)
        e1, o1 = self.split(ref[row, f, 1], far_of(f, 1), slot, spare)
        return [e0, e1, o0, o1]

    def own(self, ref, strip_ref, r, f):
        group, slot = divmod(r, SEGS)
        return self.tiles(ref, r, lambda f, par: strip_ref[group, f, par], slot, False, f)

    def beyond(self, ref, corner, dist, f, near):
        slot = (dist - 1) % SEGS
        if not near:
            slot = SEGS - 1 - slot
        far = corner if dist < DEPTH else (lambda f, par: None)
        return self.tiles(ref, dist - 1, far, slot, dist > SEGS, f)


def row_coefs(w):
    sub, _ = iotas()
    out = {name: [None] * n for name, n in TILES.items() if name != "ce"}
    lat = [None] * 4
    for par in range(2):
        even, odd = w[par], w[2 + par]
        out["cl"][par] = conduct(even, odd, 0.5)
        lat[2 + par] = conduct(odd, north(even), 0.5)
        lat[par] = south(lat[2 + par])
    out["cn"] = list(lat)
    for side in range(2):
        even, odd = w[2 * side], w[2 * side + 1]
        out["ca"][side] = conduct(even, odd, 0.5 * vert_ratio)
        above = jnp.where(sub == SUB - 1, 0.0, up(even))
        cb = conduct(odd, above, 0.5 * vert_ratio)
        out["cb"][2 * side : 2 * side + 2] = [down(cb), cb]
    for t in range(4):
        hw = w[t] * (helm_shift / HALF) + (lat[t] + out["cb"][t])
        out["hw"][t] = hw
        out["d0"][t] = MU - hw
        out["d1"][t] = 2.0 * MU - hw
    return out


def sweep(span, step, read, write, coef):
    turn, stage = divmod(step - 1, EVERY)
    first = span[0]
    before, now = read(step - 1, first - 1), read(step - 1, first)
    last_flux = [coef("ce", first - 1, t) * (now[t] - before[t]) for t in range(4)]
    for r in span:
        ahead = read(step - 1, r + 1)
        flux = [coef("ce", r, t) * (ahead[t] - now[t]) for t in range(4)]
        acc = [flux[t] - last_flux[t] for t in range(4)]
        for par in range(2):
            even, odd = now[par], now[2 + par]
            fl = coef("cl", r, par) * (odd - even)
            acc[par] = acc[par] + (coef("cn", r, par) * south(odd) + fl)
            acc[2 + par] = acc[2 + par] + (coef("cn", r, 2 + par) * north(even) - fl)
        for s in range(2):
            even, odd = now[2 * s], now[2 * s + 1]
            fa = coef("ca", r, s) * (odd - even)
            acc[2 * s] = acc[2 * s] + (coef("cb", r, 2 * s) * down(odd) + fa)
            acc[2 * s + 1] = acc[2 * s + 1] + (coef("cb", r, 2 * s + 1) * up(even) - fa)
        v = read(turn * EVERY + (stage < CHEB), r) if stage >= CHEB - 1 else None
        out = []
        for t in range(4):
            if stage == 0:
                y = acc[t] + coef("d1", r, t) * now[t]
            elif stage < CHEB:
                y = acc[t] + coef("d0", r, t) * now[t]
                if stage == CHEB - 1:
                    y = y + NU * v[t]
            else:
                y = v[t] - STEP * (coef("hw", r, t) * now[t] - acc[t])
            out.append(y)
        write(step, r, out)
        now, last_flux = ahead, flux


class Moments:
    def __init__(self):
        self.acc = [[None] * 4 for _ in range(2 * ITERS)]

    def add(self, j, x, y):
        for t in range(4):
            term = x[t] * y[t]
            self.acc[j][t] = term if self.acc[j][t] is None else self.acc[j][t] + term

    def step(self, step, r, tiles, read):
        turn, stage = divmod(step - 1, EVERY)
        if stage == CHEB - 1:
            self.add(2 * turn, tiles, read(turn * EVERY, r))
        elif stage == CHEB:
            self.add(2 * turn + 1, tiles, read(step - 1, r))

    def total(self, j):
        a, b, c, d = self.acc[j]
        return (a + b) + (c + d)


def first_u(rows, k):
    return rows - (k * EVERY + CHEB), rows - (k + 1) * EVERY


def near_kernel(place_ref, tile_ref, near_ref, corner_ref, *refs):
    rows = tile_ref.shape[1]
    edge_ref, kept_ref, u_ref, r_ref, part_ref = refs[:5]
    coef_refs = dict(zip(NAMES, refs[5:13]))
    w_ref, v_ref, p_ref, q_ref = refs[13:]
    lanes = Lanes(place_ref[0] % 2)
    bufs = (v_ref, p_ref, q_ref, p_ref)

    def read(step, r):
        return [bufs[step % EVERY][r + DEPTH, t] for t in range(4)]

    def coef(name, r, t):
        return coef_refs[name][r + DEPTH, t]

    sums = Moments()

    def write(step, r, tiles):
        spread(bufs[step % EVERY], (r + DEPTH,), tiles)

    def keep(step):
        turn, stage = divmod(step - 1, EVERY)
        first = max(rows - EVERY - step, -DEPTH + step)
        for r in range(first, rows - step):
            tiles = read(step, r)
            if r >= rows - 2 - step:
                spread(edge_ref, (step, r - (rows - 2 - step)), tiles)
            if step % EVERY == 0:
                spread(kept_ref, (step // EVERY, r - (rows - EVERY - step)), tiles)

    for f, ref in enumerate((w_ref, v_ref)):
        for r in range(-DEPTH, rows):
            if r < 0:
                tiles = lanes.beyond(near_ref, lambda f, par: corner_ref[f, par], -r, f, True)
            else:
                tiles = [tile_ref[f, r, t] for t in range(4)]
            spread(ref, (r + DEPTH,), tiles)
    fill_coefs(coef_refs, w_ref)
    keep(0)
    for step in range(1, DEPTH + 1):
        turn, stage = divmod(step - 1, EVERY)
        sweep(range(step - DEPTH, rows - step), step, read, write, coef)
        if step < DEPTH:
            keep(step)
        for r in range(rows - step):
            tiles = read(step, r)
            if stage == CHEB - 1:
                spread(u_ref, (turn, r), tiles)
            elif stage == CHEB:
                spread(r_ref, (turn, r), tiles)
            sums.step(step, r, tiles, read)
    for j in range(2 * ITERS):
        part_ref[j] = sums.total(j)


def fill_coefs(coef_refs, w_ref):
    total = w_ref.shape[0]
    for k in range(total):
        w = [w_ref[k, t] for t in range(4)]
        for name, tiles in row_coefs(w).items():
            spread(coef_refs[name], (k,), tiles)
        if k < total - 1:
            spread(coef_refs["ce"], (k,), [conduct(w[t], w_ref[k + 1, t], 0.5) for t in range(4)])


def coef_scratch(total):
    return [pltpu.VMEM((total, TILES[name], SUB, LANES), jnp.float32) for name in NAMES]


def near_side(place, tiles, near, corner):
    rows = tiles.shape[1]
    vmem = pl.BlockSpec(memory_space=pltpu.VMEM)
    outs = [tiles_of(DEPTH, 2, 4), tiles_of(ITERS, EVERY, 4)]
    outs += [tiles_of(ITERS, rows, 4)] * 2 + [tiles_of(2 * ITERS)]
    full = [pltpu.VMEM((rows + DEPTH, 4, SUB, LANES), jnp.float32)] * 4
    return pl.pallas_call(
        near_kernel,
        out_shape=outs,
        in_specs=[pl.BlockSpec(memory_space=pltpu.SMEM)] + [vmem] * 3,
        out_specs=[vmem] * len(outs),
        scratch_shapes=coef_scratch(rows + DEPTH) + full,
        compiler_params=pltpu.CompilerParams(vmem_limit_bytes=16 * MIB),
        cost_estimate=pl.CostEstimate(flops=20000000, bytes_accessed=4 * MIB, transcendentals=0),
        name="near_side",
    )(place, tiles, near, corner)


def far_kernel(place_ref, tile_ref, far_ref, corner_ref, edge_ref, kept_ref, part_in_ref, *refs):
    u_ref, r_ref, part_ref = refs[:3]
    coef_refs = dict(zip(NAMES, refs[3:11]))
    w_ref, v_ref, p_ref, q_ref = refs[11:]
    rows = tile_ref.shape[1]
    base = rows - DEPTH - 1
    lanes = Lanes(place_ref[0] % 2)
    sub, lane = iotas()
    bufs = (v_ref, p_ref, q_ref, p_ref)

    def read(step, r):
        if r >= rows - step:
            return [bufs[step % EVERY][r, t] for t in range(4)]
        if r >= rows - 2 - step:
            return [edge_ref[step, r - (rows - 2 - step), t] for t in range(4)]
        return [kept_ref[step // EVERY, r - (rows - EVERY - step), t] for t in range(4)]

    def coef(name, r, t):
        return coef_refs[name][r - base, t]

    sums = Moments()

    def write(step, r, tiles):
        spread(bufs[step % EVERY], (r,), tiles)

    for r in range(base, rows + DEPTH):
        if r < rows:
            w = [tile_ref[0, r, t] for t in range(4)]
        else:
            w, v = (
                lanes.beyond(far_ref, lambda f, par: corner_ref[f, par], r - rows + 1, f, False) for f in range(2)
            )
            spread(v_ref, (r,), v)
        spread(w_ref, (r - base,), w)
    fill_coefs(coef_refs, w_ref)
    for step in range(1, DEPTH + 1):
        turn, stage = divmod(step - 1, EVERY)
        sweep(range(rows - step, rows + DEPTH - step), step, read, write, coef)
        for r in range(rows - step, rows):
            tiles = read(step, r)
            if stage == CHEB - 1:
                spread(u_ref, (turn, r), tiles)
            elif stage == CHEB:
                spread(r_ref, (turn, r), tiles)
            sums.step(step, r, tiles, read)
    block = jnp.zeros((SUB, LANES), jnp.float32)
    for j in range(2 * ITERS):
        part = jnp.where(lanes.left, sums.total(j) + part_in_ref[j], 0.0)
        block = jnp.where(sub == j, jnp.sum(part, axis=0, keepdims=True), block)
    block = jnp.broadcast_to(jnp.sum(block, axis=1, keepdims=True), (SUB, LANES))
    row = jnp.sum(jnp.where(sub == lane, block, 0.0), axis=0, keepdims=True)
    row = jnp.broadcast_to(row, (SUB, LANES))
    for n in range(0, part_ref.shape[0], SUB):
        part_ref[n : n + SUB, :] = row


def far_side(place, tiles, far, corner, edge, kept, part, peers):
    rows = tiles.shape[1]
    vmem = pl.BlockSpec(memory_space=pltpu.VMEM)
    outs = [tiles_of(ITERS, rows, 4)] * 2 + [jax.ShapeDtypeStruct((peers, LANES), jnp.float32)]
    full = [pltpu.VMEM((2 * DEPTH + 1, 4, SUB, LANES), jnp.float32)]
    full += [pltpu.VMEM((rows + DEPTH, 4, SUB, LANES), jnp.float32)] * 3
    return pl.pallas_call(
        far_kernel,
        out_shape=outs,
        in_specs=[pl.BlockSpec(memory_space=pltpu.SMEM)] + [vmem] * 6,
        out_specs=[vmem] * 3,
        scratch_shapes=coef_scratch(2 * DEPTH + 1) + full,
        compiler_params=pltpu.CompilerParams(vmem_limit_bytes=16 * MIB),
        cost_estimate=pl.CostEstimate(flops=15000000, bytes_accessed=4 * MIB, transcendentals=0),
        name="far_side",
    )(place, tiles, far, corner, edge, kept, part)


def times_t(poly):
    out = [poly[0]]
    for i in range(1, len(poly)):
        out.append(poly[i] - poly[i - 1])
    out.append(-poly[-1])
    return out


def add_scaled(left, factor, right):
    out = []
    for i in range(max(len(left), len(right))):
        if i >= len(right):
            out.append(left[i])
        elif i >= len(left):
            out.append(factor * right[i])
        else:
            out.append(left[i] + factor * right[i])
    return out


def inner(left, right, moments):
    total = None
    for i, x in enumerate(left):
        for j, y in enumerate(right):
            term = x * y * moments[i + j]
            total = term if total is None else total + term
    return total


def last_kernel(place_ref, sums_ref, own_ref, u_near_ref, r_near_ref, u_far_ref, r_far_ref, sol_ref, res_ref):
    rows = own_ref.shape[0]
    flip = place_ref[0] // 2
    acc = sums_ref[:SUB, :]
    for n in range(SUB, sums_ref.shape[0], SUB):
        acc = acc + sums_ref[n : n + SUB, :]
    acc = jnp.sum(acc, axis=0, keepdims=True)
    moments = [jnp.broadcast_to(acc[:, j : j + 1], (SUB, LANES)) for j in range(2 * ITERS)]
    res = [jnp.ones((SUB, LANES), jnp.float32)]
    direction = res
    sol = None
    gamma = alpha = None
    for turn in range(ITERS):
        gamma_now = inner(res, res, moments)
        delta = inner(times_t(res), res, moments)
        if turn == 0:
            alpha = gamma_now / delta
            sol = [alpha]
        else:
            beta = gamma_now / gamma
            alpha = gamma_now / (delta - beta * gamma_now / alpha)
            direction = add_scaled(res, beta, direction)
            sol = add_scaled(sol, alpha, direction)
        res = add_scaled(res, -alpha, times_t(direction))
        gamma = gamma_now
    sol = [x * (STEP / HALF) for x in sol]
    _, lane = iotas()
    left = lane < WIDE
    mixed = WIDE * (lane % 2) + lane // 2
    for i in range(rows):
        u_refs, r_refs = [], []
        for k in range(ITERS):
            n_u, n_r = first_u(rows, k)
            u_refs.append(u_near_ref if i < n_u else u_far_ref)
            r_refs.append(r_near_ref if i < n_r else r_far_ref)
        for par in range(2):
            at = pl.ds(par * rows + column(rows, i, flip), SUB, stride=2 * rows)
            pair = []
            for t in (par, 2 + par):
                x = sol[0] * u_refs[0][0, i, t]
                y = res[1] * r_refs[0][0, i, t]
                for k in range(1, ITERS):
                    x = x + sol[k] * u_refs[k][k, i, t]
                    y = y + res[k + 1] * r_refs[k][k, i, t]
                pair.append((x, y))
            x, y = (jnp.where(left, even, pltpu.roll(odd, WIDE, 1)) for even, odd in zip(*pair))
            x = take_lanes(x, mixed)
            y = take_lanes(y + res[0] * own_ref[i, 1, par], mixed)
            sol_ref[at, :] = x
            res_ref[at, :] = y


def last(place, sums, own, *vectors):
    rows = own.shape[0]
    vmem = pl.BlockSpec(memory_space=pltpu.VMEM)
    out = jax.ShapeDtypeStruct((2 * SUB * rows, LANES), jnp.float32)
    return pl.pallas_call(
        last_kernel,
        out_shape=(out, out),
        in_specs=[pl.BlockSpec(memory_space=pltpu.SMEM)] + [vmem] * (2 + len(vectors)),
        out_specs=(vmem,) * 2,
        compiler_params=pltpu.CompilerParams(vmem_limit_bytes=48 * MIB),
        name="combine",
    )(place, sums, own, *vectors)


def local(right_side, scale, land_mask, bottom):
    levels, rows, lats = right_side.shape
    lon = lax.axis_size("lon")
    lat = lax.axis_size("lat")
    peers = lon * lat
    assert levels == 2 * SUB and lats == LANES and lat == 2
    assert rows == 2 * SEGS and rows >= DEPTH and 2 * EDGE >= DEPTH
    assert lon % 2 == 0 and peers % SUB == 0
    both = ("lon", "lat")

    def links(to):
        return [(i * lat + j, to(i, j)[0] % lon * lat + to(i, j)[1]) for i in range(lon) for j in range(lat)]

    beyond = lambda i: i + 1 if i % 2 else i - 1
    place = lax.axis_index("lat") + 2 * (1 - lax.axis_index("lon") % 2)
    place = place.astype(jnp.int32).reshape(1)
    fields = jnp.stack([scale, right_side]).reshape(2 * levels * rows, lats)
    own, strip, near, corner = prep(place, fields, land_mask, bottom)
    corner = lax.ppermute(corner, both, links(lambda i, j: (i ^ 1, 1 - j)))
    near = lax.ppermute(near, both, links(lambda i, j: (i ^ 1, j)))
    strip = lax.ppermute(strip, both, links(lambda i, j: (i, 1 - j)))
    far_corner, far, tiles = pack(place, own, strip, corner)
    far = lax.ppermute(far, both, links(lambda i, j: (beyond(i), j)))
    far_corner = lax.ppermute(far_corner, both, links(lambda i, j: (beyond(i), j)))
    edge, kept, u_near, r_near, part = near_side(place, tiles, near, corner)
    u_far, r_far, parts = far_side(place, tiles, far, far_corner, edge, kept, part, peers)
    sums = lax.all_to_all(parts, both, 0, 0, tiled=True)
    sol, res = last(place, sums, own, u_near, r_near, u_far, r_far)
    return sol.reshape(right_side.shape), res.reshape(right_side.shape)


def solution(mesh):
    field = P("member", "lon", "lat")
    mask = P(("member", "lon"), "lat")
    return jax.shard_map(
        local,
        mesh=mesh,
        in_specs=(field, field, mask, mask),
        out_specs=(field, field),
        check_vma=False,
    )
```

```python
import functools

import jax
import jax.numpy as jnp
from jax import lax
from jax.experimental import pallas as pl
from jax.experimental.pallas import tpu as pltpu
from jax.sharding import PartitionSpec as P

ITERS = 3
CHEB = 3
DEPTH = ITERS * (CHEB + 1)
SUB = 8
LANES = 128
WIDE = LANES // 2
SEGS = 8
EDGE = WIDE // SEGS

helm_shift = 0.05
vert_ratio = 4.0
cheb_low = 4.0
cheb_high = 150.0

CENTRE = 0.5 * (cheb_high + cheb_low)
HALF = 0.5 * (cheb_high - cheb_low)
MU = CENTRE / HALF
NU = MU * MU - 1.0
STEP = 5.0
NAMES = ("ce", "cn", "cl", "ca", "cb", "d1", "d0", "hw")
TILES = dict(ce=4, cn=4, cl=2, ca=2, cb=4, d1=4, d0=4, hw=4)
EVERY = CHEB + 1
SPARE = 2
MIB = 1024 * 1024


def take_lanes(x, index):
    return jnp.take_along_axis(x, index, axis=1, mode="promise_in_bounds")


def spread(ref, index, tiles):
    for t, tile in enumerate(tiles):
        ref[index + (t,)] = tile


def iotas():
    sub = lax.broadcasted_iota(jnp.int32, (SUB, LANES), 0)
    lane = lax.broadcasted_iota(jnp.int32, (SUB, LANES), 1)
    return sub, lane


def either(flip, x, mirrored):
    return jnp.where(jnp.broadcast_to(flip, x.shape) == 1, mirrored, x)


def spare_lanes(core):
    _, lane = iotas()
    back = lax.rem(EDGE - SPARE + core * (LANES - 2 * (EDGE - SPARE)), LANES)
    start = (1 - core) * (EDGE - SPARE)
    in_slot = lane % EDGE
    return (in_slot >= start) & (in_slot < start + SPARE), back


def prep_kernel(place_ref, both_ref, land_ref, bottom_ref, own_ref, strip_ref, near_ref, corner_ref):
    rows = own_ref.shape[0]
    core, flip = place_ref[0] % 2, place_ref[0] // 2
    sub, lane = iotas()
    half_lane = lane % WIDE
    apart = 2 * half_lane + lane // WIDE
    packed = {}
    for r in range(rows):
        group, seg = divmod(r, SEGS)
        shift = lax.rem(EDGE * seg + (1 - core) * (WIDE + EDGE), LANES)
        pair = (r, rows - 1 - r)
        deep = either(flip, *(jnp.where(land_ref[i : i + 1, :] == 1, bottom_ref[i : i + 1, :], 0) for i in pair))
        deep = jnp.broadcast_to(deep, (SUB, LANES))
        for par in range(2):
            wet = 2 * sub + par < deep
            for f in range(2):
                start = (2 * SUB * f + par) * rows
                x = either(flip, *(both_ref[pl.ds(start + i, SUB, stride=2 * rows), :] for i in pair))
                x = take_lanes(jnp.where(wet, x, 0.0), apart)
                own_ref[r, f, par] = x
                if r < DEPTH:
                    near_ref[r, f, par] = x
                y = pltpu.roll(x, shift, 1)
                if seg:
                    y = jnp.where(half_lane >= EDGE * seg, y, packed[group, f, par])
                packed[group, f, par] = y
    for (group, f, par), y in packed.items():
        strip_ref[group, f, par] = y
    spare, back = spare_lanes(1 - core)
    for f in range(2):
        for par in range(2):
            first, second = packed[0, f, par], packed[1, f, par]
            corner_ref[f, par] = jnp.where(spare, pltpu.roll(second, back, 1), first)


def prep(place, fields, land, bottom):
    rows = land.shape[0]
    vmem = pl.BlockSpec(memory_space=pltpu.VMEM)
    return pl.pallas_call(
        prep_kernel,
        out_shape=(tiles_of(rows, 2, 2), tiles_of(rows // SEGS, 2, 2), tiles_of(DEPTH, 2, 2), tiles_of(2, 2)),
        in_specs=[pl.BlockSpec(memory_space=pltpu.SMEM)] + [vmem] * 3,
        out_specs=(vmem,) * 4,
        compiler_params=pltpu.CompilerParams(vmem_limit_bytes=8 * MIB),
        name="prep",
    )(place, fields, land, bottom)


def pack_kernel(place_ref, own_ref, strip_ref, near_corner_ref, far_corner_ref, far_ref, tile_ref):
    rows = own_ref.shape[0]
    spare, back = spare_lanes(place_ref[0] % 2)
    for f in range(2):
        for par in range(2):
            for dist in range(1, DEPTH + 1):
                far_ref[dist - 1, f, par] = own_ref[rows - dist, f, par]
            first, second = strip_ref[0, f, par], strip_ref[1, f, par]
            far_corner_ref[f, par] = jnp.where(spare, pltpu.roll(first, back, 1), second)
    lanes = Lanes(place_ref[0] % 2)
    for f in range(2):
        for r in range(rows):
            spread(tile_ref, (f, r), lanes.own(own_ref, strip_ref, r, f))


def pack(place, own, strip, corner):
    vmem = pl.BlockSpec(memory_space=pltpu.VMEM)
    return pl.pallas_call(
        pack_kernel,
        out_shape=(tiles_of(2, 2), tiles_of(DEPTH, 2, 2), tiles_of(2, own.shape[0], 4)),
        in_specs=[pl.BlockSpec(memory_space=pltpu.SMEM)] + [vmem] * 3,
        out_specs=(vmem,) * 3,
        compiler_params=pltpu.CompilerParams(vmem_limit_bytes=8 * MIB),
        cost_estimate=pl.CostEstimate(flops=20000000, bytes_accessed=16 * MIB, transcendentals=0),
        name="pack",
    )(place, own, strip, corner)


def tiles_of(*n):
    return jax.ShapeDtypeStruct(n + (SUB, LANES), jnp.float32)


def conduct(x, y, factor):
    return jnp.where(jnp.minimum(x, y) > 0.0, (x + y) * (factor / HALF), 0.0)


def north(x):
    return pltpu.roll(x, LANES - 1, 1)


def south(x):
    return pltpu.roll(x, 1, 1)


def up(x):
    return pltpu.roll(x, SUB - 1, 0)


def down(x):
    return pltpu.roll(x, 1, 0)


class Lanes:
    def __init__(self, core):
        sub, lane = iotas()
        self.core = core
        self.base = WIDE + core * (WIDE - EDGE)
        self.left = lane < WIDE
        self.in_even = (lane >= self.base) & (lane < self.base + EDGE)
        self.in_odd = (lane >= self.base - WIDE) & (lane < self.base - WIDE + EDGE)

    def split(self, near, far, slot, spare=False):
        if far is None:
            even, odd = jnp.where(self.left, near, 0.0), jnp.where(self.left, 0.0, near)
        else:
            shift = self.base + (LANES - EDGE * slot)
            if spare:
                shift = shift + (LANES - (EDGE - SPARE)) + 2 * self.core * (EDGE - SPARE)
            far = pltpu.roll(far, lax.rem(shift, LANES), 1)
            even = jnp.where(self.left, near, jnp.where(self.in_even, far, 0.0))
            odd = jnp.where(self.left, jnp.where(self.in_odd, far, 0.0), near)
        return even, pltpu.roll(odd, WIDE, 1)

    def tiles(self, ref, row, far_of, slot, spare, f):
        e0, o0 = self.split(ref[row, f, 0], far_of(f, 0), slot, spare)
        e1, o1 = self.split(ref[row, f, 1], far_of(f, 1), slot, spare)
        return [e0, e1, o0, o1]

    def own(self, ref, strip_ref, r, f):
        group, slot = divmod(r, SEGS)
        return self.tiles(ref, r, lambda f, par: strip_ref[group, f, par], slot, False, f)

    def beyond(self, ref, corner, dist, f, near):
        slot = (dist - 1) % SEGS
        if not near:
            slot = SEGS - 1 - slot
        far = corner if dist < DEPTH else (lambda f, par: None)
        return self.tiles(ref, dist - 1, far, slot, dist > SEGS, f)


def row_coefs(w):
    sub, _ = iotas()
    out = {name: [None] * n for name, n in TILES.items() if name != "ce"}
    lat = [None] * 4
    for par in range(2):
        even, odd = w[par], w[2 + par]
        out["cl"][par] = conduct(even, odd, 0.5)
        lat[2 + par] = conduct(odd, north(even), 0.5)
        lat[par] = south(lat[2 + par])
    out["cn"] = list(lat)
    for side in range(2):
        even, odd = w[2 * side], w[2 * side + 1]
        out["ca"][side] = conduct(even, odd, 0.5 * vert_ratio)
        above = jnp.where(sub == SUB - 1, 0.0, up(even))
        cb = conduct(odd, above, 0.5 * vert_ratio)
        out["cb"][2 * side : 2 * side + 2] = [down(cb), cb]
    for t in range(4):
        hw = w[t] * (helm_shift / HALF) + (lat[t] + out["cb"][t])
        out["hw"][t] = hw
        out["d0"][t] = MU - hw
        out["d1"][t] = 2.0 * MU - hw
    return out


def sweep(span, step, read, write, coef):
    turn, stage = divmod(step - 1, EVERY)
    first = span[0]
    before, now = read(step - 1, first - 1), read(step - 1, first)
    last_flux = [coef("ce", first - 1, t) * (now[t] - before[t]) for t in range(4)]
    for r in span:
        ahead = read(step - 1, r + 1)
        flux = [coef("ce", r, t) * (ahead[t] - now[t]) for t in range(4)]
        acc = [flux[t] - last_flux[t] for t in range(4)]
        for par in range(2):
            even, odd = now[par], now[2 + par]
            fl = coef("cl", r, par) * (odd - even)
            acc[par] = acc[par] + (coef("cn", r, par) * south(odd) + fl)
            acc[2 + par] = acc[2 + par] + (coef("cn", r, 2 + par) * north(even) - fl)
        for s in range(2):
            even, odd = now[2 * s], now[2 * s + 1]
            fa = coef("ca", r, s) * (odd - even)
            acc[2 * s] = acc[2 * s] + (coef("cb", r, 2 * s) * down(odd) + fa)
            acc[2 * s + 1] = acc[2 * s + 1] + (coef("cb", r, 2 * s + 1) * up(even) - fa)
        v = read(turn * EVERY + (stage < CHEB), r) if stage >= CHEB - 1 else None
        out = []
        for t in range(4):
            if stage == 0:
                y = acc[t] + coef("d1", r, t) * now[t]
            elif stage < CHEB:
                y = acc[t] + coef("d0", r, t) * now[t]
                if stage == CHEB - 1:
                    y = y + NU * v[t]
            else:
                y = v[t] - STEP * (coef("hw", r, t) * now[t] - acc[t])
            out.append(y)
        write(step, r, out)
        now, last_flux = ahead, flux


class Moments:
    def __init__(self):
        self.acc = [[None] * 4 for _ in range(2 * ITERS)]

    def add(self, j, x, y):
        for t in range(4):
            term = x[t] * y[t]
            self.acc[j][t] = term if self.acc[j][t] is None else self.acc[j][t] + term

    def step(self, step, r, tiles, read):
        turn, stage = divmod(step - 1, EVERY)
        if stage == CHEB - 1:
            self.add(2 * turn, tiles, read(turn * EVERY, r))
        elif stage == CHEB:
            self.add(2 * turn + 1, tiles, read(step - 1, r))

    def total(self, j):
        a, b, c, d = self.acc[j]
        return (a + b) + (c + d)


def first_u(rows, k):
    return rows - (k * EVERY + CHEB), rows - (k + 1) * EVERY


def near_kernel(place_ref, tile_ref, near_ref, corner_ref, *refs):
    rows = tile_ref.shape[1]
    edge_ref, kept_ref, u_ref, r_ref, part_ref = refs[:5]
    coef_refs = dict(zip(NAMES, refs[5:13]))
    w_ref, v_ref, p_ref, q_ref = refs[13:]
    lanes = Lanes(place_ref[0] % 2)
    bufs = (v_ref, p_ref, q_ref, p_ref)

    def read(step, r):
        return [bufs[step % EVERY][r + DEPTH, t] for t in range(4)]

    def coef(name, r, t):
        return coef_refs[name][r + DEPTH, t]

    sums = Moments()

    def write(step, r, tiles):
        spread(bufs[step % EVERY], (r + DEPTH,), tiles)

    def keep(step):
        turn, stage = divmod(step - 1, EVERY)
        first = max(rows - EVERY - step, -DEPTH + step)
        for r in range(first, rows - step):
            tiles = read(step, r)
            if r >= rows - 2 - step:
                spread(edge_ref, (step, r - (rows - 2 - step)), tiles)
            if step % EVERY == 0:
                spread(kept_ref, (step // EVERY, r - (rows - EVERY - step)), tiles)

    for f, ref in enumerate((w_ref, v_ref)):
        for r in range(-DEPTH, rows):
            if r < 0:
                tiles = lanes.beyond(near_ref, lambda f, par: corner_ref[f, par], -r, f, True)
            else:
                tiles = [tile_ref[f, r, t] for t in range(4)]
            spread(ref, (r + DEPTH,), tiles)
    fill_coefs(coef_refs, w_ref)
    keep(0)
    for step in range(1, DEPTH + 1):
        turn, stage = divmod(step - 1, EVERY)
        sweep(range(step - DEPTH, rows - step), step, read, write, coef)
        if step < DEPTH:
            keep(step)
        for r in range(rows - step):
            tiles = read(step, r)
            if stage == CHEB - 1:
                spread(u_ref, (turn, r), tiles)
            elif stage == CHEB:
                spread(r_ref, (turn, r), tiles)
            sums.step(step, r, tiles, read)
    for j in range(2 * ITERS):
        part_ref[j] = sums.total(j)


def fill_coefs(coef_refs, w_ref):
    total = w_ref.shape[0]
    for k in range(total):
        w = [w_ref[k, t] for t in range(4)]
        for name, tiles in row_coefs(w).items():
            spread(coef_refs[name], (k,), tiles)
        if k < total - 1:
            spread(coef_refs["ce"], (k,), [conduct(w[t], w_ref[k + 1, t], 0.5) for t in range(4)])


def coef_scratch(total):
    return [pltpu.VMEM((total, TILES[name], SUB, LANES), jnp.float32) for name in NAMES]


def near_side(place, tiles, near, corner):
    rows = tiles.shape[1]
    vmem = pl.BlockSpec(memory_space=pltpu.VMEM)
    outs = [tiles_of(DEPTH, 2, 4), tiles_of(ITERS, EVERY, 4)]
    outs += [tiles_of(ITERS, rows, 4)] * 2 + [tiles_of(2 * ITERS)]
    full = [pltpu.VMEM((rows + DEPTH, 4, SUB, LANES), jnp.float32)] * 4
    return pl.pallas_call(
        near_kernel,
        out_shape=outs,
        in_specs=[pl.BlockSpec(memory_space=pltpu.SMEM)] + [vmem] * 3,
        out_specs=[vmem] * len(outs),
        scratch_shapes=coef_scratch(rows + DEPTH) + full,
        compiler_params=pltpu.CompilerParams(vmem_limit_bytes=16 * MIB),
        cost_estimate=pl.CostEstimate(flops=20000000, bytes_accessed=4 * MIB, transcendentals=0),
        name="near_side",
    )(place, tiles, near, corner)


def far_kernel(place_ref, tile_ref, far_ref, corner_ref, edge_ref, kept_ref, part_in_ref, *refs):
    u_ref, r_ref, part_ref = refs[:3]
    coef_refs = dict(zip(NAMES, refs[3:11]))
    w_ref, v_ref, p_ref, q_ref = refs[11:]
    rows = tile_ref.shape[1]
    base = rows - DEPTH - 1
    lanes = Lanes(place_ref[0] % 2)
    sub, lane = iotas()
    bufs = (v_ref, p_ref, q_ref, p_ref)

    def read(step, r):
        if r >= rows - step:
            return [bufs[step % EVERY][r, t] for t in range(4)]
        if r >= rows - 2 - step:
            return [edge_ref[step, r - (rows - 2 - step), t] for t in range(4)]
        return [kept_ref[step // EVERY, r - (rows - EVERY - step), t] for t in range(4)]

    def coef(name, r, t):
        return coef_refs[name][r - base, t]

    sums = Moments()

    def write(step, r, tiles):
        spread(bufs[step % EVERY], (r,), tiles)

    for r in range(base, rows + DEPTH):
        if r < rows:
            w = [tile_ref[0, r, t] for t in range(4)]
        else:
            w, v = (
                lanes.beyond(far_ref, lambda f, par: corner_ref[f, par], r - rows + 1, f, False) for f in range(2)
            )
            spread(v_ref, (r,), v)
        spread(w_ref, (r - base,), w)
    fill_coefs(coef_refs, w_ref)
    for step in range(1, DEPTH + 1):
        turn, stage = divmod(step - 1, EVERY)
        sweep(range(rows - step, rows + DEPTH - step), step, read, write, coef)
        for r in range(rows - step, rows):
            tiles = read(step, r)
            if stage == CHEB - 1:
                spread(u_ref, (turn, r), tiles)
            elif stage == CHEB:
                spread(r_ref, (turn, r), tiles)
            sums.step(step, r, tiles, read)
    block = jnp.zeros((SUB, LANES), jnp.float32)
    for j in range(2 * ITERS):
        part = jnp.where(lanes.left, sums.total(j) + part_in_ref[j], 0.0)
        block = jnp.where(sub == j, jnp.sum(part, axis=0, keepdims=True), block)
    block = jnp.broadcast_to(jnp.sum(block, axis=1, keepdims=True), (SUB, LANES))
    row = jnp.sum(jnp.where(sub == lane, block, 0.0), axis=0, keepdims=True)
    row = jnp.broadcast_to(row, (SUB, LANES))
    for n in range(0, part_ref.shape[0], SUB):
        part_ref[n : n + SUB, :] = row


def far_side(place, tiles, far, corner, edge, kept, part, peers):
    rows = tiles.shape[1]
    vmem = pl.BlockSpec(memory_space=pltpu.VMEM)
    outs = [tiles_of(ITERS, rows, 4)] * 2 + [jax.ShapeDtypeStruct((peers, LANES), jnp.float32)]
    full = [pltpu.VMEM((2 * DEPTH + 1, 4, SUB, LANES), jnp.float32)]
    full += [pltpu.VMEM((rows + DEPTH, 4, SUB, LANES), jnp.float32)] * 3
    return pl.pallas_call(
        far_kernel,
        out_shape=outs,
        in_specs=[pl.BlockSpec(memory_space=pltpu.SMEM)] + [vmem] * 6,
        out_specs=[vmem] * 3,
        scratch_shapes=coef_scratch(2 * DEPTH + 1) + full,
        compiler_params=pltpu.CompilerParams(vmem_limit_bytes=16 * MIB),
        cost_estimate=pl.CostEstimate(flops=15000000, bytes_accessed=4 * MIB, transcendentals=0),
        name="far_side",
    )(place, tiles, far, corner, edge, kept, part)


def times_t(poly):
    out = [poly[0]]
    for i in range(1, len(poly)):
        out.append(poly[i] - poly[i - 1])
    out.append(-poly[-1])
    return out


def add_scaled(left, factor, right):
    out = []
    for i in range(max(len(left), len(right))):
        if i >= len(right):
            out.append(left[i])
        elif i >= len(left):
            out.append(factor * right[i])
        else:
            out.append(left[i] + factor * right[i])
    return out


def inner(left, right, moments):
    total = None
    for i, x in enumerate(left):
        for j, y in enumerate(right):
            term = x * y * moments[i + j]
            total = term if total is None else total + term
    return total


def last_kernel(place_ref, sums_ref, own_ref, u_near_ref, r_near_ref, u_far_ref, r_far_ref, sol_ref, res_ref):
    rows = own_ref.shape[0]
    flip = place_ref[0] // 2
    acc = sums_ref[:SUB, :]
    for n in range(SUB, sums_ref.shape[0], SUB):
        acc = acc + sums_ref[n : n + SUB, :]
    acc = jnp.sum(acc, axis=0, keepdims=True)
    moments = [jnp.broadcast_to(acc[:, j : j + 1], (SUB, LANES)) for j in range(2 * ITERS)]
    res = [jnp.ones((SUB, LANES), jnp.float32)]
    direction = res
    sol = None
    gamma = alpha = None
    for turn in range(ITERS):
        gamma_now = inner(res, res, moments)
        delta = inner(times_t(res), res, moments)
        if turn == 0:
            alpha = gamma_now / delta
            sol = [alpha]
        else:
            beta = gamma_now / gamma
            alpha = gamma_now / (delta - beta * gamma_now / alpha)
            direction = add_scaled(res, beta, direction)
            sol = add_scaled(sol, alpha, direction)
        res = add_scaled(res, -alpha, times_t(direction))
        gamma = gamma_now
    sol = [x * (STEP / HALF) for x in sol]
    _, lane = iotas()
    left = lane < WIDE
    mixed = WIDE * (lane % 2) + lane // 2
    made = {}
    for i in sorted(range(rows), key=lambda i: min(i, rows - 1 - i)):
        u_refs, r_refs = [], []
        for k in range(ITERS):
            n_u, n_r = first_u(rows, k)
            u_refs.append(u_near_ref if i < n_u else u_far_ref)
            r_refs.append(r_near_ref if i < n_r else r_far_ref)
        for par in range(2):
            pair = []
            for t in (par, 2 + par):
                x = sol[0] * u_refs[0][0, i, t]
                y = res[1] * r_refs[0][0, i, t]
                for k in range(1, ITERS):
                    x = x + sol[k] * u_refs[k][k, i, t]
                    y = y + res[k + 1] * r_refs[k][k, i, t]
                pair.append((x, y))
            x, y = (jnp.where(left, even, pltpu.roll(odd, WIDE, 1)) for even, odd in zip(*pair))
            x = take_lanes(x, mixed)
            y = take_lanes(y + res[0] * own_ref[i, 1, par], mixed)
            made[i, par] = x, y
            other = rows - 1 - i
            if (other, par) in made:
                for r, mirror in ((i, other), (other, i)):
                    at = pl.ds(par * rows + r, SUB, stride=2 * rows)
                    for ref, a, b in zip((sol_ref, res_ref), made[r, par], made[mirror, par]):
                        ref[at, :] = either(flip, a, b)


def last(place, sums, own, *vectors):
    rows = own.shape[0]
    vmem = pl.BlockSpec(memory_space=pltpu.VMEM)
    out = jax.ShapeDtypeStruct((2 * SUB * rows, LANES), jnp.float32)
    return pl.pallas_call(
        last_kernel,
        out_shape=(out, out),
        in_specs=[pl.BlockSpec(memory_space=pltpu.SMEM)] + [vmem] * (2 + len(vectors)),
        out_specs=(vmem,) * 2,
        compiler_params=pltpu.CompilerParams(vmem_limit_bytes=48 * MIB),
        name="combine",
    )(place, sums, own, *vectors)


def local(right_side, scale, land_mask, bottom):
    levels, rows, lats = right_side.shape
    lon = lax.axis_size("lon")
    lat = lax.axis_size("lat")
    peers = lon * lat
    assert levels == 2 * SUB and lats == LANES and lat == 2
    assert rows == 2 * SEGS and rows >= DEPTH and 2 * EDGE >= DEPTH
    assert lon % 2 == 0 and peers % SUB == 0
    both = ("lon", "lat")

    def links(to):
        return [(i * lat + j, to(i, j)[0] % lon * lat + to(i, j)[1]) for i in range(lon) for j in range(lat)]

    beyond = lambda i: i + 1 if i % 2 else i - 1
    place = lax.axis_index("lat") + 2 * (1 - lax.axis_index("lon") % 2)
    place = place.astype(jnp.int32).reshape(1)
    fields = jnp.stack([scale, right_side]).reshape(2 * levels * rows, lats)
    own, strip, near, corner = prep(place, fields, land_mask, bottom)
    corner = lax.ppermute(corner, both, links(lambda i, j: (i ^ 1, 1 - j)))
    near = lax.ppermute(near, both, links(lambda i, j: (i ^ 1, j)))
    strip = lax.ppermute(strip, both, links(lambda i, j: (i, 1 - j)))
    far_corner, far, tiles = pack(place, own, strip, corner)
    far = lax.ppermute(far, both, links(lambda i, j: (beyond(i), j)))
    far_corner = lax.ppermute(far_corner, both, links(lambda i, j: (beyond(i), j)))
    edge, kept, u_near, r_near, part = near_side(place, tiles, near, corner)
    u_far, r_far, parts = far_side(place, tiles, far, far_corner, edge, kept, part, peers)
    sums = lax.all_to_all(parts, both, 0, 0, tiled=True)
    sol, res = last(place, sums, own, u_near, r_near, u_far, r_far)
    return sol.reshape(right_side.shape), res.reshape(right_side.shape)


def solution(mesh):
    field = P("member", "lon", "lat")
    mask = P(("member", "lon"), "lat")
    return jax.shard_map(
        local,
        mesh=mesh,
        in_specs=(field, field, mask, mask),
        out_specs=(field, field),
        check_vma=False,
    )
```

```python
import functools

import jax
import jax.numpy as jnp
from jax import lax
from jax.experimental import pallas as pl
from jax.experimental.pallas import tpu as pltpu
from jax.sharding import PartitionSpec as P

ITERS = 3
CHEB = 3
DEPTH = ITERS * (CHEB + 1)
SUB = 8
LANES = 128
WIDE = LANES // 2
SEGS = 8
EDGE = WIDE // SEGS

helm_shift = 0.05
vert_ratio = 4.0
cheb_low = 4.0
cheb_high = 150.0

CENTRE = 0.5 * (cheb_high + cheb_low)
HALF = 0.5 * (cheb_high - cheb_low)
MU = CENTRE / HALF
NU = MU * MU - 1.0
STEP = 5.0
NAMES = ("ce", "cn", "cl", "ca", "cb", "d1", "d0", "hw")
TILES = dict(ce=4, cn=4, cl=2, ca=2, cb=4, d1=4, d0=4, hw=4)
EVERY = CHEB + 1
SPARE = 2
MIB = 1024 * 1024


def take_lanes(x, index):
    return jnp.take_along_axis(x, index, axis=1, mode="promise_in_bounds")


def spread(ref, index, tiles):
    for t, tile in enumerate(tiles):
        ref[index + (t,)] = tile


def iotas():
    sub = lax.broadcasted_iota(jnp.int32, (SUB, LANES), 0)
    lane = lax.broadcasted_iota(jnp.int32, (SUB, LANES), 1)
    return sub, lane


def either(flip, x, mirrored):
    return jnp.where(jnp.broadcast_to(flip, x.shape) == 1, mirrored, x)


def spare_lanes(core):
    _, lane = iotas()
    back = lax.rem(EDGE - SPARE + core * (LANES - 2 * (EDGE - SPARE)), LANES)
    start = (1 - core) * (EDGE - SPARE)
    in_slot = lane % EDGE
    return (in_slot >= start) & (in_slot < start + SPARE), back


def prep_kernel(place_ref, both_ref, land_ref, bottom_ref, own_ref, strip_ref, near_ref, corner_ref):
    rows = own_ref.shape[0]
    core, flip = place_ref[0] % 2, place_ref[0] // 2
    sub, lane = iotas()
    half_lane = lane % WIDE
    apart = 2 * half_lane + lane // WIDE
    packed = {}
    for r in range(rows):
        group, seg = divmod(r, SEGS)
        shift = lax.rem(EDGE * seg + (1 - core) * (WIDE + EDGE), LANES)
        pair = (r, rows - 1 - r)
        deep = either(flip, *(jnp.where(land_ref[i : i + 1, :] == 1, bottom_ref[i : i + 1, :], 0) for i in pair))
        deep = jnp.broadcast_to(deep, (SUB, LANES))
        for par in range(2):
            wet = 2 * sub + par < deep
            for f in range(2):
                start = (2 * SUB * f + par) * rows
                x = either(flip, *(both_ref[pl.ds(start + i, SUB, stride=2 * rows), :] for i in pair))
                x = take_lanes(jnp.where(wet, x, 0.0), apart)
                own_ref[r, f, par] = x
                if r < DEPTH:
                    near_ref[r, f, par] = x
                y = pltpu.roll(x, shift, 1)
                if seg:
                    y = jnp.where(half_lane >= EDGE * seg, y, packed[group, f, par])
                packed[group, f, par] = y
    for (group, f, par), y in packed.items():
        strip_ref[group, f, par] = y
    spare, back = spare_lanes(1 - core)
    for f in range(2):
        for par in range(2):
            first, second = packed[0, f, par], packed[1, f, par]
            corner_ref[f, par] = jnp.where(spare, pltpu.roll(second, back, 1), first)


def prep(place, fields, land, bottom):
    rows = land.shape[0]
    vmem = pl.BlockSpec(memory_space=pltpu.VMEM)
    return pl.pallas_call(
        prep_kernel,
        out_shape=(tiles_of(rows, 2, 2), tiles_of(rows // SEGS, 2, 2), tiles_of(DEPTH, 2, 2), tiles_of(2, 2)),
        in_specs=[pl.BlockSpec(memory_space=pltpu.SMEM)] + [vmem] * 3,
        out_specs=(vmem,) * 4,
        compiler_params=pltpu.CompilerParams(vmem_limit_bytes=8 * MIB),
        name="prep",
    )(place, fields, land, bottom)


def pack_kernel(place_ref, own_ref, strip_ref, near_corner_ref, far_corner_ref, far_ref, tile_ref):
    rows = own_ref.shape[0]
    spare, back = spare_lanes(place_ref[0] % 2)
    for f in range(2):
        for par in range(2):
            for dist in range(1, DEPTH + 1):
                far_ref[dist - 1, f, par] = own_ref[rows - dist, f, par]
            first, second = strip_ref[0, f, par], strip_ref[1, f, par]
            far_corner_ref[f, par] = jnp.where(spare, pltpu.roll(first, back, 1), second)
    lanes = Lanes(place_ref[0] % 2)
    for f in range(2):
        for r in range(rows):
            spread(tile_ref, (f, r), lanes.own(own_ref, strip_ref, r, f))


def pack(place, own, strip, corner):
    vmem = pl.BlockSpec(memory_space=pltpu.VMEM)
    return pl.pallas_call(
        pack_kernel,
        out_shape=(tiles_of(2, 2), tiles_of(DEPTH, 2, 2), tiles_of(2, own.shape[0], 4)),
        in_specs=[pl.BlockSpec(memory_space=pltpu.SMEM)] + [vmem] * 3,
        out_specs=(vmem,) * 3,
        compiler_params=pltpu.CompilerParams(vmem_limit_bytes=8 * MIB),
        cost_estimate=pl.CostEstimate(flops=20000000, bytes_accessed=16 * MIB, transcendentals=0),
        name="pack",
    )(place, own, strip, corner)


def tiles_of(*n):
    return jax.ShapeDtypeStruct(n + (SUB, LANES), jnp.float32)


def conduct(x, y, factor):
    return jnp.where(jnp.minimum(x, y) > 0.0, (x + y) * (factor / HALF), 0.0)


def north(x):
    return pltpu.roll(x, LANES - 1, 1)


def south(x):
    return pltpu.roll(x, 1, 1)


def up(x):
    return pltpu.roll(x, SUB - 1, 0)


def down(x):
    return pltpu.roll(x, 1, 0)


class Lanes:
    def __init__(self, core):
        sub, lane = iotas()
        self.core = core
        self.base = WIDE + core * (WIDE - EDGE)
        self.left = lane < WIDE
        self.in_even = (lane >= self.base) & (lane < self.base + EDGE)
        self.in_odd = (lane >= self.base - WIDE) & (lane < self.base - WIDE + EDGE)

    def split(self, near, far, slot, spare=False):
        if far is None:
            even, odd = jnp.where(self.left, near, 0.0), jnp.where(self.left, 0.0, near)
        else:
            shift = self.base + (LANES - EDGE * slot)
            if spare:
                shift = shift + (LANES - (EDGE - SPARE)) + 2 * self.core * (EDGE - SPARE)
            far = pltpu.roll(far, lax.rem(shift, LANES), 1)
            even = jnp.where(self.left, near, jnp.where(self.in_even, far, 0.0))
            odd = jnp.where(self.left, jnp.where(self.in_odd, far, 0.0), near)
        return even, pltpu.roll(odd, WIDE, 1)

    def tiles(self, ref, row, far_of, slot, spare, f):
        e0, o0 = self.split(ref[row, f, 0], far_of(f, 0), slot, spare)
        e1, o1 = self.split(ref[row, f, 1], far_of(f, 1), slot, spare)
        return [e0, e1, o0, o1]

    def own(self, ref, strip_ref, r, f):
        group, slot = divmod(r, SEGS)
        return self.tiles(ref, r, lambda f, par: strip_ref[group, f, par], slot, False, f)

    def beyond(self, ref, corner, dist, f, near):
        slot = (dist - 1) % SEGS
        if not near:
            slot = SEGS - 1 - slot
        far = corner if dist < DEPTH else (lambda f, par: None)
        return self.tiles(ref, dist - 1, far, slot, dist > SEGS, f)


def row_coefs(w):
    sub, _ = iotas()
    out = {name: [None] * n for name, n in TILES.items() if name != "ce"}
    lat = [None] * 4
    for par in range(2):
        even, odd = w[par], w[2 + par]
        out["cl"][par] = conduct(even, odd, 0.5)
        lat[2 + par] = conduct(odd, north(even), 0.5)
        lat[par] = south(lat[2 + par])
    out["cn"] = list(lat)
    for side in range(2):
        even, odd = w[2 * side], w[2 * side + 1]
        out["ca"][side] = conduct(even, odd, 0.5 * vert_ratio)
        above = jnp.where(sub == SUB - 1, 0.0, up(even))
        cb = conduct(odd, above, 0.5 * vert_ratio)
        out["cb"][2 * side : 2 * side + 2] = [down(cb), cb]
    for t in range(4):
        hw = w[t] * (helm_shift / HALF) + (lat[t] + out["cb"][t])
        out["hw"][t] = hw
        out["d0"][t] = MU - hw
        out["d1"][t] = 2.0 * MU - hw
    return out


def sweep(span, step, read, write, coef):
    turn, stage = divmod(step - 1, EVERY)
    first = span[0]
    before, now = read(step - 1, first - 1), read(step - 1, first)
    last_flux = [coef("ce", first - 1, t) * (now[t] - before[t]) for t in range(4)]
    for r in span:
        ahead = read(step - 1, r + 1)
        flux = [coef("ce", r, t) * (ahead[t] - now[t]) for t in range(4)]
        acc = [flux[t] - last_flux[t] for t in range(4)]
        for par in range(2):
            even, odd = now[par], now[2 + par]
            fl = coef("cl", r, par) * (odd - even)
            acc[par] = acc[par] + (coef("cn", r, par) * south(odd) + fl)
            acc[2 + par] = acc[2 + par] + (coef("cn", r, 2 + par) * north(even) - fl)
        for s in range(2):
            even, odd = now[2 * s], now[2 * s + 1]
            fa = coef("ca", r, s) * (odd - even)
            acc[2 * s] = acc[2 * s] + (coef("cb", r, 2 * s) * down(odd) + fa)
            acc[2 * s + 1] = acc[2 * s + 1] + (coef("cb", r, 2 * s + 1) * up(even) - fa)
        v = read(turn * EVERY + (stage < CHEB), r) if stage >= CHEB - 1 else None
        out = []
        for t in range(4):
            if stage == 0:
                y = acc[t] + coef("d1", r, t) * now[t]
            elif stage < CHEB:
                y = acc[t] + coef("d0", r, t) * now[t]
                if stage == CHEB - 1:
                    y = y + NU * v[t]
            else:
                y = v[t] - STEP * (coef("hw", r, t) * now[t] - acc[t])
            out.append(y)
        write(step, r, out)
        now, last_flux = ahead, flux


class Moments:
    def __init__(self):
        self.acc = [[None] * 4 for _ in range(2 * ITERS)]

    def add(self, j, x, y):
        for t in range(4):
            term = x[t] * y[t]
            self.acc[j][t] = term if self.acc[j][t] is None else self.acc[j][t] + term

    def step(self, step, r, tiles, read):
        turn, stage = divmod(step - 1, EVERY)
        if stage == CHEB - 1:
            self.add(2 * turn, tiles, read(turn * EVERY, r))
        elif stage == CHEB:
            self.add(2 * turn + 1, tiles, read(step - 1, r))

    def total(self, j):
        a, b, c, d = self.acc[j]
        return (a + b) + (c + d)


def first_u(rows, k):
    return rows - (k * EVERY + CHEB), rows - (k + 1) * EVERY


def near_kernel(place_ref, tile_ref, near_ref, corner_ref, *refs):
    rows = tile_ref.shape[1]
    edge_ref, kept_ref, u_ref, r_ref, part_ref = refs[:5]
    coef_refs = dict(zip(NAMES, refs[5:13]))
    w_ref, v_ref, p_ref, q_ref = refs[13:]
    lanes = Lanes(place_ref[0] % 2)
    bufs = (v_ref, p_ref, q_ref, p_ref)

    def read(step, r):
        return [bufs[step % EVERY][r + DEPTH, t] for t in range(4)]

    def coef(name, r, t):
        return coef_refs[name][r + DEPTH, t]

    sums = Moments()

    def write(step, r, tiles):
        spread(bufs[step % EVERY], (r + DEPTH,), tiles)
        turn, stage = divmod(step - 1, EVERY)
        if 0 <= r < rows and stage >= CHEB - 1:
            spread(u_ref if stage == CHEB - 1 else r_ref, (turn, r), tiles)

    def keep(step):
        turn, stage = divmod(step - 1, EVERY)
        first = max(rows - EVERY - step, -DEPTH + step)
        for r in range(first, rows - step):
            tiles = read(step, r)
            if r >= rows - 2 - step:
                spread(edge_ref, (step, r - (rows - 2 - step)), tiles)
            if step % EVERY == 0:
                spread(kept_ref, (step // EVERY, r - (rows - EVERY - step)), tiles)

    for f, ref in enumerate((w_ref, v_ref)):
        for r in range(-DEPTH, rows):
            if r < 0:
                tiles = lanes.beyond(near_ref, lambda f, par: corner_ref[f, par], -r, f, True)
            else:
                tiles = [tile_ref[f, r, t] for t in range(4)]
            spread(ref, (r + DEPTH,), tiles)
    fill_coefs(coef_refs, w_ref)
    keep(0)
    for step in range(1, DEPTH + 1):
        turn, stage = divmod(step - 1, EVERY)
        sweep(range(step - DEPTH, rows - step), step, read, write, coef)
        if step < DEPTH:
            keep(step)
        for r in range(rows - step):
            sums.step(step, r, read(step, r), read)
    for j in range(2 * ITERS):
        part_ref[j] = sums.total(j)


def fill_coefs(coef_refs, w_ref):
    total = w_ref.shape[0]
    for k in range(total):
        w = [w_ref[k, t] for t in range(4)]
        for name, tiles in row_coefs(w).items():
            spread(coef_refs[name], (k,), tiles)
        if k < total - 1:
            spread(coef_refs["ce"], (k,), [conduct(w[t], w_ref[k + 1, t], 0.5) for t in range(4)])


def coef_scratch(total):
    return [pltpu.VMEM((total, TILES[name], SUB, LANES), jnp.float32) for name in NAMES]


def near_side(place, tiles, near, corner):
    rows = tiles.shape[1]
    vmem = pl.BlockSpec(memory_space=pltpu.VMEM)
    outs = [tiles_of(DEPTH, 2, 4), tiles_of(ITERS, EVERY, 4)]
    outs += [tiles_of(ITERS, rows, 4)] * 2 + [tiles_of(2 * ITERS)]
    full = [pltpu.VMEM((rows + DEPTH, 4, SUB, LANES), jnp.float32)] * 4
    return pl.pallas_call(
        near_kernel,
        out_shape=outs,
        in_specs=[pl.BlockSpec(memory_space=pltpu.SMEM)] + [vmem] * 3,
        out_specs=[vmem] * len(outs),
        scratch_shapes=coef_scratch(rows + DEPTH) + full,
        compiler_params=pltpu.CompilerParams(vmem_limit_bytes=16 * MIB),
        cost_estimate=pl.CostEstimate(flops=20000000, bytes_accessed=4 * MIB, transcendentals=0),
        name="near_side",
    )(place, tiles, near, corner)


def far_kernel(place_ref, tile_ref, far_ref, corner_ref, edge_ref, kept_ref, part_in_ref, *refs):
    u_ref, r_ref, part_ref = refs[:3]
    coef_refs = dict(zip(NAMES, refs[3:11]))
    w_ref, v_ref, p_ref, q_ref = refs[11:]
    rows = tile_ref.shape[1]
    base = rows - DEPTH - 1
    lanes = Lanes(place_ref[0] % 2)
    sub, lane = iotas()
    bufs = (v_ref, p_ref, q_ref, p_ref)

    def read(step, r):
        if r >= rows - step:
            return [bufs[step % EVERY][r, t] for t in range(4)]
        if r >= rows - 2 - step:
            return [edge_ref[step, r - (rows - 2 - step), t] for t in range(4)]
        return [kept_ref[step // EVERY, r - (rows - EVERY - step), t] for t in range(4)]

    def coef(name, r, t):
        return coef_refs[name][r - base, t]

    sums = Moments()

    def write(step, r, tiles):
        spread(bufs[step % EVERY], (r,), tiles)
        turn, stage = divmod(step - 1, EVERY)
        if 0 <= r < rows and stage >= CHEB - 1:
            spread(u_ref if stage == CHEB - 1 else r_ref, (turn, r), tiles)

    for r in range(base, rows + DEPTH):
        if r < rows:
            w = [tile_ref[0, r, t] for t in range(4)]
        else:
            w, v = (
                lanes.beyond(far_ref, lambda f, par: corner_ref[f, par], r - rows + 1, f, False) for f in range(2)
            )
            spread(v_ref, (r,), v)
        spread(w_ref, (r - base,), w)
    fill_coefs(coef_refs, w_ref)
    for step in range(1, DEPTH + 1):
        turn, stage = divmod(step - 1, EVERY)
        sweep(range(rows - step, rows + DEPTH - step), step, read, write, coef)
        for r in range(rows - step, rows):
            sums.step(step, r, read(step, r), read)
    block = jnp.zeros((SUB, LANES), jnp.float32)
    for j in range(2 * ITERS):
        part = jnp.where(lanes.left, sums.total(j) + part_in_ref[j], 0.0)
        block = jnp.where(sub == j, jnp.sum(part, axis=0, keepdims=True), block)
    block = jnp.broadcast_to(jnp.sum(block, axis=1, keepdims=True), (SUB, LANES))
    row = jnp.sum(jnp.where(sub == lane, block, 0.0), axis=0, keepdims=True)
    row = jnp.broadcast_to(row, (SUB, LANES))
    for n in range(0, part_ref.shape[0], SUB):
        part_ref[n : n + SUB, :] = row


def far_side(place, tiles, far, corner, edge, kept, part, peers):
    rows = tiles.shape[1]
    vmem = pl.BlockSpec(memory_space=pltpu.VMEM)
    outs = [tiles_of(ITERS, rows, 4)] * 2 + [jax.ShapeDtypeStruct((peers, LANES), jnp.float32)]
    full = [pltpu.VMEM((2 * DEPTH + 1, 4, SUB, LANES), jnp.float32)]
    full += [pltpu.VMEM((rows + DEPTH, 4, SUB, LANES), jnp.float32)] * 3
    return pl.pallas_call(
        far_kernel,
        out_shape=outs,
        in_specs=[pl.BlockSpec(memory_space=pltpu.SMEM)] + [vmem] * 6,
        out_specs=[vmem] * 3,
        scratch_shapes=coef_scratch(2 * DEPTH + 1) + full,
        compiler_params=pltpu.CompilerParams(vmem_limit_bytes=16 * MIB),
        cost_estimate=pl.CostEstimate(flops=15000000, bytes_accessed=4 * MIB, transcendentals=0),
        name="far_side",
    )(place, tiles, far, corner, edge, kept, part)


def times_t(poly):
    out = [poly[0]]
    for i in range(1, len(poly)):
        out.append(poly[i] - poly[i - 1])
    out.append(-poly[-1])
    return out


def add_scaled(left, factor, right):
    out = []
    for i in range(max(len(left), len(right))):
        if i >= len(right):
            out.append(left[i])
        elif i >= len(left):
            out.append(factor * right[i])
        else:
            out.append(left[i] + factor * right[i])
    return out


def inner(left, right, moments):
    total = None
    for i, x in enumerate(left):
        for j, y in enumerate(right):
            term = x * y * moments[i + j]
            total = term if total is None else total + term
    return total


def last_kernel(place_ref, sums_ref, own_ref, u_near_ref, r_near_ref, u_far_ref, r_far_ref, sol_ref, res_ref):
    rows = own_ref.shape[0]
    flip = place_ref[0] // 2
    acc = sums_ref[:SUB, :]
    for n in range(SUB, sums_ref.shape[0], SUB):
        acc = acc + sums_ref[n : n + SUB, :]
    acc = jnp.sum(acc, axis=0, keepdims=True)
    moments = [jnp.broadcast_to(acc[:, j : j + 1], (SUB, LANES)) for j in range(2 * ITERS)]
    res = [jnp.ones((SUB, LANES), jnp.float32)]
    direction = res
    sol = None
    gamma = alpha = None
    for turn in range(ITERS):
        gamma_now = inner(res, res, moments)
        delta = inner(times_t(res), res, moments)
        if turn == 0:
            alpha = gamma_now / delta
            sol = [alpha]
        else:
            beta = gamma_now / gamma
            alpha = gamma_now / (delta - beta * gamma_now / alpha)
            direction = add_scaled(res, beta, direction)
            sol = add_scaled(sol, alpha, direction)
        res = add_scaled(res, -alpha, times_t(direction))
        gamma = gamma_now
    sol = [x * (STEP / HALF) for x in sol]
    _, lane = iotas()
    left = lane < WIDE
    mixed = WIDE * (lane % 2) + lane // 2
    made = {}
    for i in sorted(range(rows), key=lambda i: min(i, rows - 1 - i)):
        u_refs, r_refs = [], []
        for k in range(ITERS):
            n_u, n_r = first_u(rows, k)
            u_refs.append(u_near_ref if i < n_u else u_far_ref)
            r_refs.append(r_near_ref if i < n_r else r_far_ref)
        for par in range(2):
            pair = []
            for t in (par, 2 + par):
                x = sol[0] * u_refs[0][0, i, t]
                y = res[1] * r_refs[0][0, i, t]
                for k in range(1, ITERS):
                    x = x + sol[k] * u_refs[k][k, i, t]
                    y = y + res[k + 1] * r_refs[k][k, i, t]
                pair.append((x, y))
            x, y = (jnp.where(left, even, pltpu.roll(odd, WIDE, 1)) for even, odd in zip(*pair))
            x = take_lanes(x, mixed)
            y = take_lanes(y + res[0] * own_ref[i, 1, par], mixed)
            made[i, par] = x, y
            other = rows - 1 - i
            if (other, par) in made:
                for r, mirror in ((i, other), (other, i)):
                    at = pl.ds(par * rows + r, SUB, stride=2 * rows)
                    for ref, a, b in zip((sol_ref, res_ref), made[r, par], made[mirror, par]):
                        ref[at, :] = either(flip, a, b)


def last(place, sums, own, *vectors):
    rows = own.shape[0]
    vmem = pl.BlockSpec(memory_space=pltpu.VMEM)
    out = jax.ShapeDtypeStruct((2 * SUB * rows, LANES), jnp.float32)
    return pl.pallas_call(
        last_kernel,
        out_shape=(out, out),
        in_specs=[pl.BlockSpec(memory_space=pltpu.SMEM)] + [vmem] * (2 + len(vectors)),
        out_specs=(vmem,) * 2,
        compiler_params=pltpu.CompilerParams(vmem_limit_bytes=48 * MIB),
        name="combine",
    )(place, sums, own, *vectors)


def local(right_side, scale, land_mask, bottom):
    levels, rows, lats = right_side.shape
    lon = lax.axis_size("lon")
    lat = lax.axis_size("lat")
    peers = lon * lat
    assert levels == 2 * SUB and lats == LANES and lat == 2
    assert rows == 2 * SEGS and rows >= DEPTH and 2 * EDGE >= DEPTH
    assert lon % 2 == 0 and peers % SUB == 0
    both = ("lon", "lat")

    def links(to):
        return [(i * lat + j, to(i, j)[0] % lon * lat + to(i, j)[1]) for i in range(lon) for j in range(lat)]

    beyond = lambda i: i + 1 if i % 2 else i - 1
    place = lax.axis_index("lat") + 2 * (1 - lax.axis_index("lon") % 2)
    place = place.astype(jnp.int32).reshape(1)
    fields = jnp.stack([scale, right_side]).reshape(2 * levels * rows, lats)
    own, strip, near, corner = prep(place, fields, land_mask, bottom)
    corner = lax.ppermute(corner, both, links(lambda i, j: (i ^ 1, 1 - j)))
    near = lax.ppermute(near, both, links(lambda i, j: (i ^ 1, j)))
    strip = lax.ppermute(strip, both, links(lambda i, j: (i, 1 - j)))
    far_corner, far, tiles = pack(place, own, strip, corner)
    far = lax.ppermute(far, both, links(lambda i, j: (beyond(i), j)))
    far_corner = lax.ppermute(far_corner, both, links(lambda i, j: (beyond(i), j)))
    edge, kept, u_near, r_near, part = near_side(place, tiles, near, corner)
    u_far, r_far, parts = far_side(place, tiles, far, far_corner, edge, kept, part, peers)
    sums = lax.all_to_all(parts, both, 0, 0, tiled=True)
    sol, res = last(place, sums, own, u_near, r_near, u_far, r_far)
    return sol.reshape(right_side.shape), res.reshape(right_side.shape)


def solution(mesh):
    field = P("member", "lon", "lat")
    mask = P(("member", "lon"), "lat")
    return jax.shard_map(
        local,
        mesh=mesh,
        in_specs=(field, field, mask, mask),
        out_specs=(field, field),
        check_vma=False,
    )
```
